32 devices in a mesh: ctx: 8 (over y, x, core), exp: 4 (over z).
Axes of the slice: x: 2, y: 2, z: 4, core: 2. Of those that a mesh axis runs over, the one named last changes fastest.
Arguments:
- hidden_in: bfloat16 [1024, 2880], P('ctx'), may hold values from -6 to 6
- query_input: bfloat16 [1024, 2048], P('ctx', 'exp'), may hold values from -16 to 16
- key_heads_input: bfloat16 [1024, 256], P('ctx'), may hold values from -16 to 16
- value_heads_input: bfloat16 [1024, 256], P('ctx'), may hold values from -6 to 6
- sink_logits: float32 [32], P('exp'), may hold values from 0 to 4
- out_proj: bfloat16 [2048, 2880], P('exp'), may hold values from -0.125 to 0.125
- norm_gain: float32 [2880], replicated, may hold values from 0.5 to 1.5
- expert_ids: int32 [1024, 4], P('ctx'), may hold values from 0 to 7, all different within a row; in each aligned block of 128 rows (0 to 127, 128 to 255, ...) at most 80 rows name the same one
- expert_gates: float32 [1024, 4], P('ctx'), may hold values from 0.1 to 1
- gate_up: bfloat16 [8, 2880, 2, 2880], P('ctx', None, None, 'exp'), may hold values from -0.109375 to 0.109375
- down_proj: bfloat16 [8, 2880, 2880], P('ctx', 'exp'), may hold values from -0.109375 to 0.109375
Outputs:
- layer_out: bfloat16 [1024, 2880], P('ctx', 'exp')
The draws below stay inside these ranges and needn't reach their ends.
Inputs may be any that keep to these rules, and one draw needn't show every extreme that they name: `expert_ids`: each token names 4 different experts; within the 128 tokens of one device no expert is named by more than 80 tokens.
All inputs are finite; a program needn't handle non-finite values.
Results may differ from the reference program's by a relative error of at most 0.02.
Values may be sent and summed in bfloat16 or wider, within the bound.
A program may use at most 64 MiB of HBM per device.

```python
import math
import jax
import jax.numpy as jnp
import numpy as np
from jax import lax

D = 2880
QUERY_HEADS = 32
KEY_VALUE_HEADS = 4
HEAD_SIZE = 64
FF = 2880
TOPK = 4
BLOCK_TOKENS = 128
SEQUENCE_TOKENS = 1024
EXPERTS = 8
CAP = 80
N_CTX = 8
N_EXP = 4


def outlier_rows(key, row_count, col_count):
    base = jax.random.normal(jax.random.fold_in(key, 1), (row_count, col_count), jnp.float32)
    return jnp.clip(base, -16.0, 16.0)


def draw_query_input(key, part):
    return outlier_rows(jax.random.fold_in(key, 11), BLOCK_TOKENS * N_CTX, QUERY_HEADS * HEAD_SIZE).astype(jnp.bfloat16)


def draw_key_heads_input(key, part):
    return outlier_rows(jax.random.fold_in(key, 23), BLOCK_TOKENS * N_CTX, KEY_VALUE_HEADS * HEAD_SIZE).astype(jnp.bfloat16)


def block_levels(key, extent, split, least, high):
    level, own = 1.0, jax.random.fold_in(key, 6)
    for axis_at, parts in split:
        draws = jnp.exp(jax.random.uniform(jax.random.fold_in(own, axis_at), (parts,), jnp.float32, least / len(split), high / len(split)))
        level = level * jnp.repeat(draws, extent[axis_at] // parts).reshape([-1 if axis == axis_at else 1 for axis in range(len(extent))])
    return level


def routed_block(key, own, number, rows, amount, top, most, lean):
    sequence = jax.random.permutation(key, amount)
    heavy_load, common = shares(amount, rows * top, most, lean, True), shares(amount, rows * top, most, lean, False)
    places = jnp.arange(amount)

    def named(tallies, turn):
        used = int((tallies > 0).sum())
        fixed = max(1, used // 4)
        shifted = fixed + (places - fixed + turn * (used - fixed)) % max(1, amount - fixed)
        return jnp.zeros((amount,), jnp.int32).at[sequence[jnp.where(places < fixed, places, shifted)]].set(jnp.asarray(tallies, jnp.int32))

    tallies = jnp.where(number % 4 == 0, named(heavy_load, number // 4), named(common, number - number // 4 - 1))
    mixed = jax.random.permutation(jax.random.fold_in(own, 3), amount)
    source_of, taker = mixed[0:amount // 2 * 2:2], mixed[1:amount // 2 * 2:2]
    slack = jnp.minimum(tallies[source_of] - 1, most - tallies[taker]) // 2
    slack = jnp.where((source_of == sequence[0]) | (taker == sequence[0]) | (tallies[taker] == 0), 0, jnp.maximum(slack, 0))
    shifted = jax.random.randint(jax.random.fold_in(own, 4), (amount // 2,), 0, 1 << 20) % (slack + 1)
    tallies = tallies.at[source_of].add(-shifted).at[taker].add(shifted)
    items = jnp.searchsorted(jnp.cumsum(tallies), jnp.arange(rows * top), side="right").astype(jnp.int32)
    listing = items.reshape(top, rows).T
    listing = listing[jax.random.permutation(jax.random.fold_in(own, 1), rows)]
    turn = jax.random.randint(jax.random.fold_in(own, 2), (rows, 1), 0, top)
    return jnp.take_along_axis(listing, (jnp.arange(top)[None, :] + turn) % top, axis=1)


def shares(amount, total, limit, slope, full):
    portions = [(1 << 20) // math.isqrt(rank ** slope) + 1 for rank in range(1, amount + 1)]
    largest = limit if full else min(limit, max(-(-total // amount), total * portions[0] // sum(portions)))
    least = 1 if total - largest >= amount - 1 else 0
    counts, rest = [largest] + [least] * (amount - 1), total - largest - least * (amount - 1)
    while rest > 0:
        movable = [i for i in range(1, amount) if counts[i] < largest] or [i for i in range(1, amount) if counts[i] < limit]
        pool, remaining = sum([portions[i] for i in movable]), rest
        for i in movable:
            more = min(limit - counts[i], max(1, remaining * portions[i] // pool), rest)
            counts[i] = counts[i] + more
            rest = rest - more
    return np.array(counts)


def gaussian(stream_key, dims, width, reach, shards=(), kind=jnp.bfloat16):
    array = jax.random.normal(stream_key, dims, jnp.float32) * width
    if len(shards) > 0:
        array = block_levels(stream_key, dims, shards, -0.22, 0.18) * array
    return jnp.clip(array, min=-reach, max=reach).astype(kind)


def setup_inputs(seed: int = 0) -> dict:
    streams_of = jax.random.split(jax.random.key(seed), 12)
    hidden_in = gaussian(streams_of[0], (SEQUENCE_TOKENS, D), 1.0, 6.0, ((0, 8),))
    query_input = draw_query_input(jax.random.fold_in(streams_of[11], 71), 0)
    key_heads_input = draw_key_heads_input(jax.random.fold_in(streams_of[11], 71), 0)
    value_heads_input = gaussian(streams_of[3], (SEQUENCE_TOKENS, KEY_VALUE_HEADS * HEAD_SIZE), 1.0, 6.0, ((0, 8),))
    sink_logits = jnp.clip(4.0 * jax.random.uniform(streams_of[4], (QUERY_HEADS,), jnp.float32) ** block_levels(streams_of[4], (QUERY_HEADS,), ((0, 4),), -0.2, 0.2), 0.0, 4.0)
    out_proj = gaussian(streams_of[5], (QUERY_HEADS * HEAD_SIZE, D), (QUERY_HEADS * HEAD_SIZE) ** -0.5, 0.125, ((0, 4),))
    norm_gain = jnp.clip(1.0 + 0.1 * jax.random.normal(streams_of[6], (D,), jnp.float32), 0.5, 1.5)
    expert_ids_keys = jax.random.split(jax.random.fold_in(streams_of[7], 1), SEQUENCE_TOKENS // BLOCK_TOKENS)
    expert_ids_turns = jax.random.permutation(jax.random.fold_in(streams_of[7], 3), SEQUENCE_TOKENS // BLOCK_TOKENS)
    expert_ids = jax.vmap(lambda own, number: routed_block(jax.random.fold_in(streams_of[7], 2), own, number, BLOCK_TOKENS, EXPERTS, TOPK, CAP, 1))(expert_ids_keys, expert_ids_turns).reshape((SEQUENCE_TOKENS, TOPK))
    expert_gates = jnp.clip(0.1 + 0.9 * jax.random.uniform(streams_of[8], (SEQUENCE_TOKENS, TOPK), jnp.float32) ** block_levels(streams_of[8], (SEQUENCE_TOKENS, TOPK), ((0, 8),), -0.2, 0.2), 0.1, 1.0)
    gate_up = gaussian(streams_of[9], (EXPERTS, D, 2, FF), D ** -0.5, 0.109375, ((0, 8), (3, 4)))
    down_proj = gaussian(streams_of[10], (EXPERTS, FF, D), FF ** -0.5, 0.109375, ((0, 8), (1, 4)))
    return dict(hidden_in=hidden_in, query_input=query_input, key_heads_input=key_heads_input, value_heads_input=value_heads_input, sink_logits=sink_logits, out_proj=out_proj, norm_gain=norm_gain, expert_ids=expert_ids, expert_gates=expert_gates, gate_up=gate_up, down_proj=down_proj)


yarn_base = 150000.0
yarn_factor = 32.0
yarn_initial = 4096.0
beta_fast = 32.0
beta_slow = 1.0
neg_large = -1e+30

def yarn_frequencies(head_dim):
    half_dim = head_dim // 2

    def correction(rotations):
        return head_dim * math.log(yarn_initial / (rotations * 2.0 * math.pi)) / (2.0 * math.log(yarn_base))
    lower_dim = max(math.floor(correction(beta_fast)), 0)
    upper_dim = min(math.ceil(correction(beta_slow)), head_dim - 1)
    extrap_freq = 1.0 / yarn_base ** (np.arange(0, head_dim, 2) / head_dim)
    interp_freq = extrap_freq / yarn_factor
    ramp_part = np.clip((np.arange(half_dim) - lower_dim) / (upper_dim - lower_dim), 0.0, 1.0)
    extrap_share = 1.0 - ramp_part
    return (interp_freq * (1.0 - extrap_share) + extrap_freq * extrap_share).astype(np.float32)

def rotate_with_yarn(heads_in, token_positions):
    head_dim = heads_in.shape[-1]
    freqs = jnp.asarray(yarn_frequencies(head_dim))
    angles = token_positions.astype(jnp.float32)[:, None] * freqs[None, :]
    factor = 0.1 * math.log(yarn_factor) + 1.0
    cosine = (jnp.cos(angles) * factor)[:, None, :]
    sine = (jnp.sin(angles) * factor)[:, None, :]
    first_half = heads_in[..., :head_dim // 2]
    second_half = heads_in[..., head_dim // 2:]
    return jnp.concatenate([first_half * cosine - second_half * sine, second_half * cosine + first_half * sine], axis=-1)

def route_slots(ids_block, n_experts):
    flat_ids = ids_block.reshape(-1)
    onehot = (flat_ids[:, None] == jnp.arange(n_experts, dtype=jnp.int32)[None, :]).astype(jnp.int32)
    ranks = jnp.cumsum(onehot, axis=0) - onehot
    return lax.optimization_barrier(jnp.sum(ranks * onehot, axis=1)).astype(jnp.int32).reshape(ids_block.shape)

def reference(hidden_in, query_input, key_heads_input, value_heads_input, sink_logits, out_proj, norm_gain, expert_ids, expert_gates, gate_up, down_proj):
    sequence_length = hidden_in.shape[0]
    token_positions = jnp.arange(sequence_length, dtype=jnp.int32)
    q_rot = rotate_with_yarn(query_input.astype(jnp.float32).reshape(sequence_length, QUERY_HEADS, HEAD_SIZE), token_positions).astype(jnp.bfloat16)
    rotated_keys = rotate_with_yarn(key_heads_input.astype(jnp.float32).reshape(sequence_length, KEY_VALUE_HEADS, HEAD_SIZE), token_positions).astype(jnp.bfloat16)
    value_heads = value_heads_input.reshape(sequence_length, KEY_VALUE_HEADS, HEAD_SIZE)
    query_group_width = QUERY_HEADS // KEY_VALUE_HEADS
    causal = token_positions[:, None] >= token_positions[None, :]
    score_scale = 1.0 / math.sqrt(HEAD_SIZE)

    def one_head(head):
        shared_key_head = head // query_group_width
        q_head = lax.dynamic_index_in_dim(q_rot, head, 1, keepdims=False)
        k_head = lax.dynamic_index_in_dim(rotated_keys, shared_key_head, 1, keepdims=False)
        v_head = lax.dynamic_index_in_dim(value_heads, shared_key_head, 1, keepdims=False).astype(jnp.float32)
        scores = jnp.dot(q_head, k_head.T, preferred_element_type=jnp.float32) * score_scale
        scores = jnp.where(causal, scores, neg_large)
        sink_value = sink_logits[head]
        row_max = jnp.maximum(lax.optimization_barrier(jnp.max(scores, axis=1)), sink_value)
        weights = jnp.exp(scores - row_max[:, None])
        row_total = lax.optimization_barrier(jnp.sum(weights, axis=1)) + jnp.exp(sink_value - row_max)
        return jnp.dot(weights, v_head, precision=lax.Precision.HIGHEST) / row_total[:, None]
    attended = lax.map(one_head, jnp.arange(QUERY_HEADS, dtype=jnp.int32))
    attended = attended.transpose(1, 0, 2).reshape(sequence_length, QUERY_HEADS * HEAD_SIZE).astype(jnp.bfloat16)
    residual = hidden_in.astype(jnp.float32) + jnp.dot(attended, out_proj, preferred_element_type=jnp.float32)
    mean_square = lax.optimization_barrier(jnp.mean(residual * residual, axis=1, keepdims=True))
    normed = (residual * lax.rsqrt(mean_square + 1e-05) * norm_gain[None, :]).astype(jnp.bfloat16)
    blocks = sequence_length // BLOCK_TOKENS
    slot_index = jax.vmap(lambda ids_block: route_slots(ids_block, EXPERTS))(expert_ids.reshape(blocks, BLOCK_TOKENS, TOPK))
    slot_index = slot_index.reshape(sequence_length, TOPK)
    block_of = (token_positions // BLOCK_TOKENS).astype(jnp.int32)[:, None]
    row_index = block_of * CAP + slot_index
    bucket_rows = blocks * CAP
    spread_rows = jnp.broadcast_to(normed[:, None, :], (sequence_length, TOPK, D))
    expert_rows = jnp.zeros((EXPERTS, bucket_rows, D), jnp.bfloat16).at[expert_ids, row_index].set(spread_rows)

    def one_expert(operands):
        rows_in, weights_gu, weights_down = operands
        gate_up_out = jnp.dot(rows_in, weights_gu.reshape(D, 2 * FF), preferred_element_type=jnp.float32).reshape(bucket_rows, 2, FF)
        gate_value = gate_up_out[:, 0]
        up_value = gate_up_out[:, 1]
        activated = ((up_value + 1.0) * gate_value * jax.nn.sigmoid(1.702 * gate_value)).astype(jnp.bfloat16)
        groups = activated.reshape(bucket_rows, N_EXP, FF // N_EXP).astype(jnp.float32)
        down_groups = weights_down.reshape(N_EXP, FF // N_EXP, D).astype(jnp.float32)
        partial_value = jnp.einsum('rsf,sfd->srd', groups, down_groups, precision=lax.Precision.HIGHEST)
        rounded = lax.optimization_barrier(partial_value.astype(jnp.bfloat16))
        return lax.optimization_barrier(jnp.sum(rounded.astype(jnp.float32), axis=0))
    expert_out = lax.map(one_expert, (expert_rows, gate_up, down_proj))
    picked_rows = expert_out[expert_ids, row_index]
    moe = lax.optimization_barrier(jnp.sum(expert_gates[:, :, None] * picked_rows, axis=1))
    return (residual + moe).astype(jnp.bfloat16)
```

```python
import math

import jax
import jax.numpy as jnp
import numpy as np
from jax import lax
from jax.sharding import PartitionSpec as P

D = 2880
QUERY_HEADS = 32
KEY_VALUE_HEADS = 4
HEAD_SIZE = 64


yarn_base = 150000.0
yarn_factor = 32.0
yarn_initial = 4096.0
beta_fast = 32.0
beta_slow = 1.0
neg_large = -1e30


def yarn_frequencies(head_dim):
    half_dim = head_dim // 2

    def correction(rotations):
        return (
            head_dim
            * math.log(yarn_initial / (rotations * 2.0 * math.pi))
            / (2.0 * math.log(yarn_base))
        )

    lower_dim = max(math.floor(correction(beta_fast)), 0)
    upper_dim = min(math.ceil(correction(beta_slow)), head_dim - 1)
    extrap_freq = 1.0 / yarn_base ** (np.arange(0, head_dim, 2) / head_dim)
    interp_freq = extrap_freq / yarn_factor
    ramp_part = np.clip((np.arange(half_dim) - lower_dim) / (upper_dim - lower_dim), 0.0, 1.0)
    extrap_share = 1.0 - ramp_part
    return (interp_freq * (1.0 - extrap_share) + extrap_freq * extrap_share).astype(np.float32)


def rotate_with_yarn(heads_in, token_positions):
    head_dim = heads_in.shape[-1]
    freqs = jnp.asarray(yarn_frequencies(head_dim))
    angles = token_positions.astype(jnp.float32)[:, None] * freqs[None, :]
    factor = 0.1 * math.log(yarn_factor) + 1.0
    cosine = (jnp.cos(angles) * factor)[:, None, :]
    sine = (jnp.sin(angles) * factor)[:, None, :]
    first_half = heads_in[..., : head_dim // 2]
    second_half = heads_in[..., head_dim // 2 :]
    return jnp.concatenate(
        [first_half * cosine - second_half * sine, second_half * cosine + first_half * sine],
        axis=-1,
    )


def routing_matrices(all_ids, all_gates, blocks, rows, capacity):
    mine = all_ids == lax.axis_index("ctx").astype(jnp.float32)
    chosen = jnp.sum(mine.astype(jnp.float32), axis=1).reshape(blocks, rows)
    gate = jnp.sum(jnp.where(mine, all_gates, 0.0), axis=1).reshape(blocks, rows)
    earlier = jnp.triu(jnp.ones((rows, rows), jnp.bfloat16), 1)
    slot = jnp.dot(chosen.astype(jnp.bfloat16), earlier, preferred_element_type=jnp.float32)
    place = jnp.arange(capacity, dtype=jnp.float32)[None, :, None]
    hit = (slot[:, None, :] == place) & (chosen[:, None, :] > 0.0)
    pick = hit.astype(jnp.bfloat16)
    weighted = jnp.where(hit, gate[:, None, :], 0.0).astype(jnp.bfloat16)
    return pick, weighted


def per_device(
    hidden_in,
    query_input,
    key_heads_input,
    value_heads_input,
    sink_logits,
    out_proj,
    norm_gain,
    expert_ids,
    expert_gates,
    gate_up,
    down_proj,
):
    tok_rows = hidden_in.shape[0]
    ctx_count = lax.axis_size("ctx")
    exp_count = lax.axis_size("exp")
    local_heads = query_input.shape[1] // HEAD_SIZE
    token_positions = lax.axis_index("ctx") * tok_rows + jnp.arange(tok_rows, dtype=jnp.int32)
    q_rot = rotate_with_yarn(
        query_input.astype(jnp.float32).reshape(tok_rows, local_heads, HEAD_SIZE), token_positions
    ).astype(jnp.bfloat16)
    shared_key_head = lax.axis_index("exp") * local_heads // (QUERY_HEADS // KEY_VALUE_HEADS)
    key_block = lax.dynamic_slice_in_dim(key_heads_input, shared_key_head * HEAD_SIZE, HEAD_SIZE, 1)
    value_block = lax.dynamic_slice_in_dim(
        value_heads_input, shared_key_head * HEAD_SIZE, HEAD_SIZE, 1
    )
    key_rot = (
        rotate_with_yarn(
            key_block.astype(jnp.float32).reshape(tok_rows, 1, HEAD_SIZE), token_positions
        )
        .reshape(tok_rows, HEAD_SIZE)
        .astype(jnp.bfloat16)
    )
    ids_part = expert_ids.astype(jnp.bfloat16)
    gate_high = expert_gates.astype(jnp.bfloat16)
    gate_low = (expert_gates - gate_high.astype(jnp.float32)).astype(jnp.bfloat16)
    top_count = expert_ids.shape[1]
    key_value = jnp.concatenate([key_rot, value_block, ids_part, gate_high, gate_low], axis=1)
    score_scale = 1.0 / math.sqrt(HEAD_SIZE)
    block_part = lax.all_gather(key_value, "ctx", axis=0, tiled=True)
    routing = block_part[:, 2 * HEAD_SIZE :].astype(jnp.float32)
    all_ids = routing[:, :top_count]
    all_gates = routing[:, top_count : 2 * top_count] + routing[:, 2 * top_count :]
    run_max = jnp.broadcast_to(sink_logits[:, None], (local_heads, tok_rows))
    run_total = jnp.ones((local_heads, tok_rows), jnp.float32)
    run_sum = jnp.zeros((local_heads, tok_rows, HEAD_SIZE), jnp.float32)
    key_count = block_part.shape[0]
    key_part = block_part[:, :HEAD_SIZE]
    value_part = block_part[:, HEAD_SIZE : 2 * HEAD_SIZE].astype(jnp.float32)
    scores = (
        jnp.einsum("rhd,kd->hrk", q_rot, key_part, preferred_element_type=jnp.float32) * score_scale
    )
    key_pos = jnp.arange(key_count, dtype=jnp.int32)
    visible = token_positions[:, None] >= key_pos[None, :]
    scores = jnp.where(visible[None, :, :], scores, neg_large)
    new_max = jnp.maximum(run_max, jnp.max(scores, axis=2))
    weights = jnp.exp(scores - new_max[:, :, None])
    factor = jnp.exp(run_max - new_max)
    run_total = run_total * factor + jnp.sum(weights, axis=2)
    run_sum = run_sum * factor[:, :, None] + jnp.einsum(
        "hrk,kd->hrd", weights, value_part, precision=lax.Precision.HIGHEST
    )
    run_max, run_total, run_sum = (new_max, run_total, run_sum)
    attended = (
        (run_sum / run_total[:, :, None])
        .transpose(1, 0, 2)
        .reshape(tok_rows, local_heads * HEAD_SIZE)
        .astype(jnp.bfloat16)
    )
    head_part = jnp.dot(attended, out_proj, preferred_element_type=jnp.float32)
    share_rows = tok_rows // exp_count
    my_row = lax.axis_index("exp") * share_rows
    residual = lax.dynamic_slice_in_dim(hidden_in, my_row, share_rows, 0).astype(
        jnp.float32
    ) + lax.psum_scatter(
        head_part.astype(jnp.bfloat16), "exp", scatter_dimension=0, tiled=True
    ).astype(jnp.float32)
    mean_square = jnp.mean(residual * residual, axis=1, keepdims=True)
    normed = (residual * lax.rsqrt(mean_square + 1e-05) * norm_gain[None, :]).astype(jnp.bfloat16)
    all_normed = lax.all_gather(normed, ("ctx", "exp"), axis=0, tiled=True)
    n_experts = gate_up.shape[0] * ctx_count
    capacity = max(2, tok_rows * top_count * 5 // (4 * n_experts))
    pick, weighted = routing_matrices(all_ids, all_gates, ctx_count, tok_rows, capacity)
    expert_rows = jnp.einsum(
        "bst,btd->bsd",
        pick,
        all_normed.reshape(ctx_count, tok_rows, D),
        preferred_element_type=jnp.float32,
    ).astype(jnp.bfloat16)
    expert_rows = expert_rows.reshape(ctx_count * capacity, D)
    unit_count = gate_up.shape[-1]
    gate_up_out = jnp.dot(
        expert_rows, gate_up.reshape(D, 2 * unit_count), preferred_element_type=jnp.float32
    )
    gate_value = gate_up_out[:, :unit_count]
    up_value = gate_up_out[:, unit_count:]
    activated = ((up_value + 1.0) * gate_value * jax.nn.sigmoid(1.702 * gate_value)).astype(
        jnp.bfloat16
    )
    partial_value = jnp.dot(
        activated, down_proj.reshape(unit_count, D), preferred_element_type=jnp.float32
    ).astype(jnp.bfloat16)
    spread = jnp.einsum(
        "bst,bsd->btd",
        weighted,
        partial_value.reshape(ctx_count, capacity, D),
        preferred_element_type=jnp.float32,
    ).astype(jnp.bfloat16)
    gated = lax.psum_scatter(
        spread.reshape(ctx_count * tok_rows, D), "ctx", scatter_dimension=0, tiled=True
    ).astype(jnp.float32)
    total = gated + lax.dynamic_update_slice_in_dim(
        jnp.zeros((tok_rows, D), jnp.float32), residual, my_row, 0
    )
    return lax.psum_scatter(
        total.astype(jnp.bfloat16), "exp", scatter_dimension=1, tiled=True
    )


def solution(mesh):
    placed = (
        P("ctx", None),
        P("ctx", "exp"),
        P("ctx", None),
        P("ctx", None),
        P("exp"),
        P("exp", None),
        P(),
        P("ctx", None),
        P("ctx", None),
        P("ctx", None, None, "exp"),
        P("ctx", "exp", None),
    )
    return jax.shard_map(
        per_device, mesh=mesh, in_specs=placed, out_specs=P("ctx", "exp"), check_vma=False
    )
```

```python
import math

import jax
import jax.numpy as jnp
import numpy as np
from jax import lax
from jax.experimental import pallas as pl
from jax.experimental.pallas import tpu as pltpu
from jax.sharding import PartitionSpec as P

D = 2880
QUERY_HEADS = 32
KEY_VALUE_HEADS = 4
HEAD_SIZE = 64


yarn_base = 150000.0
yarn_factor = 32.0
yarn_initial = 4096.0
beta_fast = 32.0
beta_slow = 1.0
neg_large = -1e30


def yarn_frequencies(head_dim):
    half_dim = head_dim // 2

    def correction(rotations):
        return (
            head_dim
            * math.log(yarn_initial / (rotations * 2.0 * math.pi))
            / (2.0 * math.log(yarn_base))
        )

    lower_dim = max(math.floor(correction(beta_fast)), 0)
    upper_dim = min(math.ceil(correction(beta_slow)), head_dim - 1)
    extrap_freq = 1.0 / yarn_base ** (np.arange(0, head_dim, 2) / head_dim)
    interp_freq = extrap_freq / yarn_factor
    ramp_part = np.clip((np.arange(half_dim) - lower_dim) / (upper_dim - lower_dim), 0.0, 1.0)
    extrap_share = 1.0 - ramp_part
    return (interp_freq * (1.0 - extrap_share) + extrap_freq * extrap_share).astype(np.float32)


def rotate_with_yarn(heads_in, token_positions):
    head_dim = heads_in.shape[-1]
    freqs = jnp.asarray(yarn_frequencies(head_dim))
    angles = token_positions.astype(jnp.float32)[:, None] * freqs[None, :]
    factor = 0.1 * math.log(yarn_factor) + 1.0
    cosine = (jnp.cos(angles) * factor)[:, None, :]
    sine = (jnp.sin(angles) * factor)[:, None, :]
    first_half = heads_in[..., : head_dim // 2]
    second_half = heads_in[..., head_dim // 2 :]
    return jnp.concatenate(
        [first_half * cosine - second_half * sine, second_half * cosine + first_half * sine],
        axis=-1,
    )


def routing_matrices(all_ids, all_gates, blocks, rows, capacity):
    mine = all_ids == lax.axis_index("ctx").astype(jnp.float32)
    chosen = jnp.sum(mine.astype(jnp.float32), axis=1).reshape(blocks, rows)
    gate = jnp.sum(jnp.where(mine, all_gates, 0.0), axis=1).reshape(blocks, rows)
    earlier = jnp.triu(jnp.ones((rows, rows), jnp.bfloat16), 1)
    slot = jnp.dot(chosen.astype(jnp.bfloat16), earlier, preferred_element_type=jnp.float32)
    place = jnp.arange(capacity, dtype=jnp.float32)[None, :, None]
    hit = (slot[:, None, :] == place) & (chosen[:, None, :] > 0.0)
    pick = hit.astype(jnp.bfloat16)
    weighted = jnp.where(hit, gate[:, None, :], 0.0).astype(jnp.bfloat16)
    return pick, weighted


PLANE_CTX = 8
PLANE_EXP = 4


def layer_kernel(
    head_ref, hidden_ref, gain_ref, pick_ref, spread_ref, gu_hbm, down_hbm, out_ref,
    gu, down, zin, residual, normed, rows, moe, core_in, first_in, second_in, total, stage, zout,
    send_sems, recv_sems, load_sems,
):
    c, e = lax.axis_index("ctx"), lax.axis_index("exp")
    y, x, k = c // 4, c // 2 % 2, c % 2
    blk = head_ref.shape[0]
    share = blk // PLANE_EXP
    half = blk // 2
    cap = pick_ref.shape[1]
    col = out_ref.shape[1]

    def at(pos, core):
        return (y + pos // 2) % 2 * 4 + (x + pos % 2) % 2 * 2 + core

    mate = at(0, 1 - k)
    ids = {}

    def copy(name, src, dst, ctx, exp):
        sem = ids.setdefault(name, len(ids))
        return pltpu.make_async_remote_copy(
            src_ref=src,
            dst_ref=dst,
            send_sem=send_sems.at[sem],
            recv_sem=recv_sems.at[sem],
            device_id=(ctx, exp),
            device_id_type=pl.DeviceIdType.MESH,
        )

    def quarter(d):
        return (e + PLANE_EXP - d) % PLANE_EXP

    def piece(ctx, d, part=None):
        first = quarter(d) * share
        if part is None:
            return normed.at[ctx, pl.ds(pl.multiple_of(first, share), share)]
        return normed.at[
            ctx, pl.ds(pl.multiple_of(first + part * (share // 2), share // 2), share // 2)
        ]

    def head_copy(d):
        peer = (e + d) % PLANE_EXP
        src = head_ref.at[pl.ds(pl.multiple_of(peer * share, share), share)]
        return copy(("head", d), src, zin.at[d], c, peer)

    def z_copy(d):
        return copy(("z", d), piece(c, 0), piece(c, 0), c, (e + d) % PLANE_EXP)

    def near_copy(pos, d):
        return copy(("near", pos, d), piece(c, d), piece(c, d), at(pos, k), e)

    def far_copy(pos, d):
        ref = piece(at(3 - pos, k), d, pos - 1)
        return copy(("far", pos, d), ref, ref, at(pos, k), e)

    def mate_copy(pos, d):
        ref = piece(at(pos, k), d)
        return copy(("mate", pos, d), ref, ref, mate, e)

    def core_copy(pos):
        return copy(("core", pos), moe.at[at(pos, 1 - k)], core_in.at[pos], mate, e)

    def first_copy(axis, pos):
        lines = pl.ds((axis - 1) * half, half)
        slot = (axis - 1) * 2 + (pos == 3)
        return copy(
            ("first", axis, pos), moe.at[at(pos, k), lines], first_in.at[slot], at(axis, k), e
        )

    def second_copy(axis):
        lines = pl.ds((2 - axis) * half, half)
        return copy(
            ("second", axis), moe.at[at(axis, k), lines], second_in.at[2 - axis], at(axis, k), e
        )

    def out_copy(d):
        peer = (e + d) % PLANE_EXP
        return copy(("out", d), stage.at[peer], zout.at[d], c, peer)

    load_gu = pltpu.make_async_copy(gu_hbm, gu, load_sems.at[0])
    load_down = pltpu.make_async_copy(down_hbm, down, load_sems.at[1])
    load_gu.start()
    load_down.start()
    barrier = pltpu.get_barrier_semaphore()
    friends = [(mate, e), (at(1, k), e), (at(2, k), e)]
    friends += [(c, (e + d) % PLANE_EXP) for d in (1, 2, 3)]
    for friend in friends:
        pl.semaphore_signal(
            barrier, inc=1, device_id=friend, device_id_type=pl.DeviceIdType.MESH
        )
    pl.semaphore_wait(barrier, len(friends))

    for d in (2, 1, 3):
        head_copy(d).start()
    own_lines = pl.ds(pl.multiple_of(e * share, share), share)
    summed = hidden_ref[...].astype(jnp.float32) + head_ref[own_lines, :].astype(jnp.float32)
    for d in (1, 3, 2):
        head_copy(d).wait_recv()
        summed = summed + zin[d].astype(jnp.float32)
    residual[...] = summed
    mean_square = jnp.mean(summed * summed, axis=1, keepdims=True)
    normed[c, own_lines, :] = (
        summed * lax.rsqrt(mean_square + 1e-05) * gain_ref[...]
    ).astype(jnp.bfloat16)

    for d in (2, 1, 3):
        z_copy(d).start()
    for d in (0, 1, 3, 2):
        if d:
            z_copy(d).wait_recv()
        near_copy(1, d).start()
        near_copy(2, d).start()
        mate_copy(0, d).start()
    for d in (0, 1, 3, 2):
        for pos in (1, 2):
            near_copy(pos, d).wait_recv()
            far_copy(3 - pos, d).start()
            mate_copy(pos, d).start()
    load_gu.wait()
    load_down.wait()

    def add_core(pos):
        core_copy(pos).wait_recv()
        mine = at(pos, k)
        moe[mine] = (moe[mine].astype(jnp.float32) + core_in[pos].astype(jnp.float32)).astype(
            jnp.bfloat16
        )

    def step(pos, carry):
        for now in range(4):

            @pl.when(pos == now)
            def _():
                if now == 2:
                    for d in range(PLANE_EXP):
                        far_copy(1, d).wait_recv()
                        far_copy(2, d).wait_recv()
                        mate_copy(3, d).start()
                for d in range(PLANE_EXP):
                    mate_copy(now, d).wait_recv()

        for core in range(2):
            block = at(pos, core)
            rows[pl.ds(core * cap, cap), :] = jnp.dot(
                pick_ref[block], normed[block], preferred_element_type=jnp.float32
            ).astype(jnp.bfloat16)
        across = (((1,), (1,)), ((), ()))
        gate = lax.dot_general(rows[...], gu[0], across, preferred_element_type=jnp.float32)
        up = lax.dot_general(rows[...], gu[1], across, preferred_element_type=jnp.float32)
        activated = ((up + 1.0) * gate * jax.nn.sigmoid(1.702 * gate)).astype(jnp.bfloat16)
        rows[...] = jnp.dot(activated, down[...], preferred_element_type=jnp.float32).astype(
            jnp.bfloat16
        )
        for core in range(2):
            block = at(pos, core)
            moe[block] = jnp.dot(
                spread_ref[block],
                rows[pl.ds(core * cap, cap), :],
                preferred_element_type=jnp.float32,
            ).astype(jnp.bfloat16)
        for now in range(4):

            @pl.when(pos == now)
            def _():
                core_copy(now).start()
                if now == 2:
                    add_core(1)
                    first_copy(1, 1).start()

        return carry

    lax.fori_loop(0, 4, step, 0)
    add_core(2)
    first_copy(2, 2).start()
    add_core(3)
    first_copy(1, 3).start()
    first_copy(2, 3).start()
    add_core(0)

    for axis in (1, 2):
        first_copy(axis, 3).wait_recv()
        lines = pl.ds((axis - 1) * half, half)
        block = at(3 - axis, k)
        moe[block, lines, :] = (
            moe[block, lines, :].astype(jnp.float32)
            + first_in[(axis - 1) * 2 + 1].astype(jnp.float32)
        ).astype(jnp.bfloat16)
        second_copy(3 - axis).start()
    for axis in (1, 2):
        first_copy(axis, axis).wait_recv()
        lines = pl.ds((axis - 1) * half, half)
        total[lines, :] = moe[c, lines, :].astype(jnp.float32) + first_in[
            (axis - 1) * 2
        ].astype(jnp.float32)
    total[own_lines, :] = total[own_lines, :] + residual[...]
    for axis in (1, 2):
        second_copy(3 - axis).wait_recv()
        lines = pl.ds((axis - 1) * half, half)
        total[lines, :] = total[lines, :] + second_in[axis - 1].astype(jnp.float32)
    for f in range(PLANE_EXP):
        stage[f] = total[:, f * col : (f + 1) * col].astype(jnp.bfloat16)
    for d in (2, 1, 3):
        out_copy(d).start()
    result = stage[e].astype(jnp.float32)
    for d in (1, 3, 2):
        out_copy(d).wait_recv()
        result = result + zout[d].astype(jnp.float32)
    out_ref[...] = result.astype(jnp.bfloat16)

    for d in (1, 2, 3):
        head_copy(d).wait_send()
        z_copy(d).wait_send()
        out_copy(d).wait_send()
    for d in range(PLANE_EXP):
        for pos in range(4):
            mate_copy(pos, d).wait_send()
        for pos in (1, 2):
            near_copy(pos, d).wait_send()
            far_copy(pos, d).wait_send()
    for pos in range(4):
        core_copy(pos).wait_send()
    for axis in (1, 2):
        first_copy(axis, axis).wait_send()
        first_copy(axis, 3).wait_send()
        second_copy(axis).wait_send()


def plane_layer(head_part, hidden_share, gain, pick, spread, gate_up, down_proj):
    blk, width = head_part.shape
    blocks, cap = pick.shape[0], pick.shape[1]
    units = gate_up.shape[-1]
    share, col = blk // PLANE_EXP, width // PLANE_EXP
    kind = jnp.bfloat16
    copies = 64
    return pl.pallas_call(
        layer_kernel,
        out_shape=jax.ShapeDtypeStruct((blk, col), kind),
        in_specs=[pl.BlockSpec(memory_space=pltpu.VMEM)] * 5
        + [pl.BlockSpec(memory_space=pl.ANY)] * 2,
        out_specs=pl.BlockSpec(memory_space=pltpu.VMEM),
        scratch_shapes=[
            pltpu.VMEM((2, units, width), kind),
            pltpu.VMEM((units, width), kind),
            pltpu.VMEM((PLANE_EXP, share, width), kind),
            pltpu.VMEM((share, width), jnp.float32),
            pltpu.VMEM((blocks, blk, width), kind),
            pltpu.VMEM((2 * cap, width), kind),
            pltpu.VMEM((blocks, blk, width), kind),
            pltpu.VMEM((4, blk, width), kind),
            pltpu.VMEM((4, blk // 2, width), kind),
            pltpu.VMEM((2, blk // 2, width), kind),
            pltpu.VMEM((blk, width), jnp.float32),
            pltpu.VMEM((PLANE_EXP, blk, col), kind),
            pltpu.VMEM((PLANE_EXP, blk, col), kind),
            pltpu.SemaphoreType.DMA((copies,)),
            pltpu.SemaphoreType.DMA((copies,)),
            pltpu.SemaphoreType.DMA((2,)),
        ],
        compiler_params=pltpu.CompilerParams(
            collective_id=0, has_side_effects=True, vmem_limit_bytes=58 * 1024 * 1024
        ),
    )(
        head_part,
        hidden_share,
        gain.reshape(1, width),
        pick,
        spread,
        gate_up[0].transpose(1, 2, 0),
        down_proj[0],
    )


def per_device(
    hidden_in,
    query_input,
    key_heads_input,
    value_heads_input,
    sink_logits,
    out_proj,
    norm_gain,
    expert_ids,
    expert_gates,
    gate_up,
    down_proj,
):
    tok_rows = hidden_in.shape[0]
    ctx_count = lax.axis_size("ctx")
    exp_count = lax.axis_size("exp")
    local_heads = query_input.shape[1] // HEAD_SIZE
    token_positions = lax.axis_index("ctx") * tok_rows + jnp.arange(tok_rows, dtype=jnp.int32)
    q_rot = rotate_with_yarn(
        query_input.astype(jnp.float32).reshape(tok_rows, local_heads, HEAD_SIZE), token_positions
    ).astype(jnp.bfloat16)
    shared_key_head = lax.axis_index("exp") * local_heads // (QUERY_HEADS // KEY_VALUE_HEADS)
    key_block = lax.dynamic_slice_in_dim(key_heads_input, shared_key_head * HEAD_SIZE, HEAD_SIZE, 1)
    value_block = lax.dynamic_slice_in_dim(
        value_heads_input, shared_key_head * HEAD_SIZE, HEAD_SIZE, 1
    )
    key_rot = (
        rotate_with_yarn(
            key_block.astype(jnp.float32).reshape(tok_rows, 1, HEAD_SIZE), token_positions
        )
        .reshape(tok_rows, HEAD_SIZE)
        .astype(jnp.bfloat16)
    )
    ids_part = expert_ids.astype(jnp.bfloat16)
    gate_high = expert_gates.astype(jnp.bfloat16)
    gate_low = (expert_gates - gate_high.astype(jnp.float32)).astype(jnp.bfloat16)
    top_count = expert_ids.shape[1]
    key_value = jnp.concatenate([key_rot, value_block, ids_part, gate_high, gate_low], axis=1)
    score_scale = 1.0 / math.sqrt(HEAD_SIZE)
    block_part = lax.all_gather(key_value, "ctx", axis=0, tiled=True)
    routing = block_part[:, 2 * HEAD_SIZE :].astype(jnp.float32)
    all_ids = routing[:, :top_count]
    all_gates = routing[:, top_count : 2 * top_count] + routing[:, 2 * top_count :]
    run_max = jnp.broadcast_to(sink_logits[:, None], (local_heads, tok_rows))
    run_total = jnp.ones((local_heads, tok_rows), jnp.float32)
    run_sum = jnp.zeros((local_heads, tok_rows, HEAD_SIZE), jnp.float32)
    key_count = block_part.shape[0]
    key_part = block_part[:, :HEAD_SIZE]
    value_part = block_part[:, HEAD_SIZE : 2 * HEAD_SIZE].astype(jnp.float32)
    scores = (
        jnp.einsum("rhd,kd->hrk", q_rot, key_part, preferred_element_type=jnp.float32) * score_scale
    )
    key_pos = jnp.arange(key_count, dtype=jnp.int32)
    visible = token_positions[:, None] >= key_pos[None, :]
    scores = jnp.where(visible[None, :, :], scores, neg_large)
    new_max = jnp.maximum(run_max, jnp.max(scores, axis=2))
    weights = jnp.exp(scores - new_max[:, :, None])
    factor = jnp.exp(run_max - new_max)
    run_total = run_total * factor + jnp.sum(weights, axis=2)
    run_sum = run_sum * factor[:, :, None] + jnp.einsum(
        "hrk,kd->hrd", weights, value_part, precision=lax.Precision.HIGHEST
    )
    run_max, run_total, run_sum = (new_max, run_total, run_sum)
    attended = (
        (run_sum / run_total[:, :, None])
        .transpose(1, 0, 2)
        .reshape(tok_rows, local_heads * HEAD_SIZE)
        .astype(jnp.bfloat16)
    )
    head_part = jnp.dot(attended, out_proj, preferred_element_type=jnp.float32)
    share_rows = tok_rows // exp_count
    my_row = lax.axis_index("exp") * share_rows
    hidden_share = lax.dynamic_slice_in_dim(hidden_in, my_row, share_rows, 0)
    n_experts = gate_up.shape[0] * ctx_count
    capacity = max(2, tok_rows * top_count * 5 // (4 * n_experts))
    pick, weighted = routing_matrices(all_ids, all_gates, ctx_count, tok_rows, capacity)
    if ctx_count == PLANE_CTX and exp_count == PLANE_EXP:
        return plane_layer(
            head_part.astype(jnp.bfloat16),
            hidden_share,
            norm_gain,
            pick,
            weighted.transpose(0, 2, 1),
            gate_up,
            down_proj,
        )
    residual = hidden_share.astype(jnp.float32) + lax.psum_scatter(
        head_part.astype(jnp.bfloat16), "exp", scatter_dimension=0, tiled=True
    ).astype(jnp.float32)
    mean_square = jnp.mean(residual * residual, axis=1, keepdims=True)
    normed = (residual * lax.rsqrt(mean_square + 1e-05) * norm_gain[None, :]).astype(jnp.bfloat16)
    all_normed = lax.all_gather(normed, ("ctx", "exp"), axis=0, tiled=True)
    expert_rows = jnp.einsum(
        "bst,btd->bsd",
        pick,
        all_normed.reshape(ctx_count, tok_rows, D),
        preferred_element_type=jnp.float32,
    ).astype(jnp.bfloat16)
    expert_rows = expert_rows.reshape(ctx_count * capacity, D)
    unit_count = gate_up.shape[-1]
    gate_up_out = jnp.dot(
        expert_rows, gate_up.reshape(D, 2 * unit_count), preferred_element_type=jnp.float32
    )
    gate_value = gate_up_out[:, :unit_count]
    up_value = gate_up_out[:, unit_count:]
    activated = ((up_value + 1.0) * gate_value * jax.nn.sigmoid(1.702 * gate_value)).astype(
        jnp.bfloat16
    )
    partial_value = jnp.dot(
        activated, down_proj.reshape(unit_count, D), preferred_element_type=jnp.float32
    ).astype(jnp.bfloat16)
    spread = jnp.einsum(
        "bst,bsd->btd",
        weighted,
        partial_value.reshape(ctx_count, capacity, D),
        preferred_element_type=jnp.float32,
    ).astype(jnp.bfloat16)
    gated = lax.psum_scatter(
        spread.reshape(ctx_count * tok_rows, D), "ctx", scatter_dimension=0, tiled=True
    ).astype(jnp.float32)
    total = gated + lax.dynamic_update_slice_in_dim(
        jnp.zeros((tok_rows, D), jnp.float32), residual, my_row, 0
    )
    return lax.psum_scatter(
        total.astype(jnp.bfloat16), "exp", scatter_dimension=1, tiled=True
    )


def solution(mesh):
    placed = (
        P("ctx", None),
        P("ctx", "exp"),
        P("ctx", None),
        P("ctx", None),
        P("exp"),
        P("exp", None),
        P(),
        P("ctx", None),
        P("ctx", None),
        P("ctx", None, None, "exp"),
        P("ctx", "exp", None),
    )
    return jax.shard_map(
        per_device, mesh=mesh, in_specs=placed, out_specs=P("ctx", "exp"), check_vma=False
    )
```

```python
import math

import jax
import jax.numpy as jnp
import numpy as np
from jax import lax
from jax.experimental import pallas as pl
from jax.experimental.pallas import tpu as pltpu
from jax.sharding import PartitionSpec as P

D = 2880
QUERY_HEADS = 32
KEY_VALUE_HEADS = 4
HEAD_SIZE = 64


yarn_base = 150000.0
yarn_factor = 32.0
yarn_initial = 4096.0
beta_fast = 32.0
beta_slow = 1.0
neg_large = -1e30


def yarn_frequencies(head_dim):
    half_dim = head_dim // 2

    def correction(rotations):
        return (
            head_dim
            * math.log(yarn_initial / (rotations * 2.0 * math.pi))
            / (2.0 * math.log(yarn_base))
        )

    lower_dim = max(math.floor(correction(beta_fast)), 0)
    upper_dim = min(math.ceil(correction(beta_slow)), head_dim - 1)
    extrap_freq = 1.0 / yarn_base ** (np.arange(0, head_dim, 2) / head_dim)
    interp_freq = extrap_freq / yarn_factor
    ramp_part = np.clip((np.arange(half_dim) - lower_dim) / (upper_dim - lower_dim), 0.0, 1.0)
    extrap_share = 1.0 - ramp_part
    return (interp_freq * (1.0 - extrap_share) + extrap_freq * extrap_share).astype(np.float32)


def rotate_with_yarn(heads_in, token_positions):
    head_dim = heads_in.shape[-1]
    freqs = jnp.asarray(yarn_frequencies(head_dim))
    angles = token_positions.astype(jnp.float32)[:, None] * freqs[None, :]
    factor = 0.1 * math.log(yarn_factor) + 1.0
    cosine = (jnp.cos(angles) * factor)[:, None, :]
    sine = (jnp.sin(angles) * factor)[:, None, :]
    first_half = heads_in[..., : head_dim // 2]
    second_half = heads_in[..., head_dim // 2 :]
    return jnp.concatenate(
        [first_half * cosine - second_half * sine, second_half * cosine + first_half * sine],
        axis=-1,
    )


def routing_matrices(all_ids, all_gates, blocks, rows, capacity):
    mine = all_ids == lax.axis_index("ctx").astype(jnp.float32)
    chosen = jnp.sum(mine.astype(jnp.float32), axis=1).reshape(blocks, rows)
    gate = jnp.sum(jnp.where(mine, all_gates, 0.0), axis=1).reshape(blocks, rows)
    earlier = jnp.triu(jnp.ones((rows, rows), jnp.bfloat16), 1)
    slot = jnp.dot(chosen.astype(jnp.bfloat16), earlier, preferred_element_type=jnp.float32)
    place = jnp.arange(capacity, dtype=jnp.float32)[None, :, None]
    hit = (slot[:, None, :] == place) & (chosen[:, None, :] > 0.0)
    pick = hit.astype(jnp.bfloat16)
    weighted = jnp.where(hit, gate[:, None, :], 0.0).astype(jnp.bfloat16)
    return pick, weighted


PLANE_CTX = 8
PLANE_EXP = 4


def layer_kernel(
    attended_ref, hidden_ref, gain_ref, pick_ref, spread_ref, proj_hbm, gu_hbm, down_hbm, out_ref,
    proj, gu, down, head, hidden, zin, residual, normed, rows, moe, core_in, first_in, corner_in, second_in, total, stage, zout,
    send_sems, recv_sems, load_sems,
):
    c, e = lax.axis_index("ctx"), lax.axis_index("exp")
    y, x, k = c // 4, c // 2 % 2, c % 2
    blk = attended_ref.shape[0]
    share = blk // PLANE_EXP
    half = blk // 2
    sub = half // 2
    cap = pick_ref.shape[1]
    col = out_ref.shape[1]

    def at(pos, core):
        return (y + pos // 2) % 2 * 4 + (x + pos % 2) % 2 * 2 + core

    mate = at(0, 1 - k)
    ids = {}

    def copy(name, src, dst, ctx, exp):
        sem = ids.setdefault(name, len(ids))
        return pltpu.make_async_remote_copy(
            src_ref=src,
            dst_ref=dst,
            send_sem=send_sems.at[sem],
            recv_sem=recv_sems.at[sem],
            device_id=(ctx, exp),
            device_id_type=pl.DeviceIdType.MESH,
        )

    def quarter(d):
        return (e + PLANE_EXP - d) % PLANE_EXP

    def piece(ctx, d, part=None):
        first = quarter(d) * share
        if part is None:
            return normed.at[ctx, pl.ds(pl.multiple_of(first, share), share)]
        return normed.at[
            ctx, pl.ds(pl.multiple_of(first + part * (share // 2), share // 2), share // 2)
        ]

    def head_copy(d):
        peer = (e + d) % PLANE_EXP
        src = head.at[pl.ds(pl.multiple_of(peer * share, share), share)]
        return copy(("head", d), src, zin.at[d], c, peer)

    def z_copy(d):
        return copy(("z", d), piece(c, 0), piece(c, 0), c, (e + d) % PLANE_EXP)

    def near_copy(pos, d):
        return copy(("near", pos, d), piece(c, d), piece(c, d), at(pos, k), e)

    def far_copy(pos, d):
        ref = piece(at(3 - pos, k), d, pos - 1)
        return copy(("far", pos, d), ref, ref, at(pos, k), e)

    def mate_copy(pos, d):
        ref = piece(at(pos, k), d)
        return copy(("mate", pos, d), ref, ref, mate, e)

    def core_copy(pos):
        return copy(("core", pos), moe.at[at(pos, 1 - k)], core_in.at[pos], mate, e)

    def lines_of(axis, part):
        return pl.ds((axis - 1) * half + part * sub, sub)

    def first_copy(axis):
        lines = pl.ds((axis - 1) * half, half)
        src = moe.at[at(axis, k), lines]
        return copy(("first", axis), src, first_in.at[axis - 1], at(axis, k), e)

    def corner_copy(axis, part):
        src = moe.at[at(3, k), lines_of(axis, part)]
        return copy(("corner", axis, part), src, corner_in.at[axis - 1, part], at(axis, k), e)

    def second_copy(axis, part):
        src = moe.at[at(axis, k), lines_of(3 - axis, part)]
        return copy(("second", axis, part), src, second_in.at[axis - 1, part], at(axis, k), e)

    def out_copy(d, part):
        peer = (e + d) % PLANE_EXP
        return copy(("out", d, part), stage.at[peer, part], zout.at[d, part], c, peer)

    load_proj = pltpu.make_async_copy(proj_hbm, proj, load_sems.at[2])
    load_proj.start()
    load_gu = pltpu.make_async_copy(gu_hbm, gu, load_sems.at[0])
    load_down = pltpu.make_async_copy(down_hbm, down, load_sems.at[1])
    barrier = pltpu.get_barrier_semaphore()
    friends = [(mate, e), (at(1, k), e), (at(2, k), e)]
    friends += [(c, (e + d) % PLANE_EXP) for d in (1, 2, 3)]
    for friend in friends:
        pl.semaphore_signal(
            barrier, inc=1, device_id=friend, device_id_type=pl.DeviceIdType.MESH
        )
    pl.semaphore_wait(barrier, len(friends))

    load_proj.wait()
    load_gu.start()
    load_down.start()
    across = (((1,), (1,)), ((), ()))
    head[...] = (
        lax.dot_general(proj[...], attended_ref[...], across, preferred_element_type=jnp.float32)
        .T.astype(jnp.bfloat16)
    )
    for d in (2, 1, 3):
        head_copy(d).start()
    hidden[...] = hidden_ref[...].astype(jnp.float32).T
    own_lines = pl.ds(pl.multiple_of(e * share, share), share)
    summed = hidden[own_lines, :] + head[own_lines, :].astype(jnp.float32)
    for d in (1, 3, 2):
        head_copy(d).wait_recv()
        summed = summed + zin[d].astype(jnp.float32)
    residual[...] = summed
    mean_square = jnp.mean(summed * summed, axis=1, keepdims=True)
    normed[c, own_lines, :] = (
        summed * lax.rsqrt(mean_square + 1e-05) * gain_ref[...]
    ).astype(jnp.bfloat16)

    for d in (2, 1, 3):
        z_copy(d).start()
    for d in (0, 1, 3, 2):
        if d:
            z_copy(d).wait_recv()
        near_copy(1, d).start()
        near_copy(2, d).start()
        mate_copy(0, d).start()
    for d in (0, 1, 3, 2):
        for pos in (1, 2):
            near_copy(pos, d).wait_recv()
            far_copy(3 - pos, d).start()
            mate_copy(pos, d).start()
    load_gu.wait()
    load_down.wait()

    def add_core(pos):
        core_copy(pos).wait_recv()
        mine = at(pos, k)
        moe[mine] = (moe[mine].astype(jnp.float32) + core_in[pos].astype(jnp.float32)).astype(
            jnp.bfloat16
        )

    def step(pos, carry):
        for now in range(4):

            @pl.when(pos == now)
            def _():
                if now == 2:
                    for d in range(PLANE_EXP):
                        far_copy(1, d).wait_recv()
                        far_copy(2, d).wait_recv()
                        mate_copy(3, d).start()
                for d in range(PLANE_EXP):
                    mate_copy(now, d).wait_recv()

        for slot, core in enumerate((1 - k, k)):
            block = at(pos, core)
            rows[slot * cap : (slot + 1) * cap, :] = jnp.dot(
                pick_ref[block], normed[block], preferred_element_type=jnp.float32
            ).astype(jnp.bfloat16)
        gate = lax.dot_general(gu[0], rows[...], across, preferred_element_type=jnp.float32)
        up = lax.dot_general(gu[1], rows[...], across, preferred_element_type=jnp.float32)
        activated = ((up + 1.0) * gate * jax.nn.sigmoid(1.702 * gate)).T.astype(jnp.bfloat16)
        rows[...] = jnp.dot(activated, down[...], preferred_element_type=jnp.float32).astype(
            jnp.bfloat16
        )
        for slot, core in enumerate((1 - k, k)):
            block = at(pos, core)
            moe[block] = jnp.dot(
                spread_ref[block],
                rows[slot * cap : (slot + 1) * cap, :],
                preferred_element_type=jnp.float32,
            ).astype(jnp.bfloat16)
            if slot == 0:
                for now in range(4):

                    @pl.when(pos == now)
                    def _():
                        core_copy(now).start()

        @pl.when(pos == 2)
        def _():
            add_core(1)
            first_copy(1).start()

        return carry

    lax.fori_loop(0, 4, step, 0)
    add_core(2)
    first_copy(2).start()
    add_core(0)
    total[...] = moe[c].astype(jnp.float32)
    total[own_lines, :] = total[own_lines, :] + residual[...]
    add_core(3)
    for part in range(2):
        for axis in (1, 2):
            corner_copy(axis, part).start()

    for part in range(2):
        for axis in (1, 2):
            corner_copy(axis, part).wait_recv()
            lines = lines_of(axis, part)
            block = at(3 - axis, k)
            moe[block, lines, :] = (
                moe[block, lines, :].astype(jnp.float32)
                + corner_in[axis - 1, part].astype(jnp.float32)
            ).astype(jnp.bfloat16)
            second_copy(3 - axis, part).start()
    for axis in (1, 2):
        first_copy(axis).wait_recv()
        lines = pl.ds((axis - 1) * half, half)
        total[lines, :] = total[lines, :] + first_in[axis - 1].astype(jnp.float32)
    for part in range(2):
        for axis in (1, 2):
            second_copy(3 - axis, part).wait_recv()
            lines = lines_of(axis, part)
            full = (total[lines, :] + second_in[2 - axis, part].astype(jnp.float32)).astype(
                jnp.bfloat16
            )
            for f in range(PLANE_EXP):
                stage[f, part, (axis - 1) * sub : axis * sub, :] = full[:, f * col : (f + 1) * col]
        for d in (2, 1, 3):
            out_copy(d, part).start()
    for part in range(2):
        result = stage[e, part].astype(jnp.float32)
        for d in (1, 3, 2):
            out_copy(d, part).wait_recv()
            result = result + zout[d, part].astype(jnp.float32)
        for axis in (1, 2):
            out_ref[lines_of(axis, part), :] = result[(axis - 1) * sub : axis * sub].astype(
                jnp.bfloat16
            )

    for d in (1, 2, 3):
        head_copy(d).wait_send()
        z_copy(d).wait_send()
        for part in range(2):
            out_copy(d, part).wait_send()
    for d in range(PLANE_EXP):
        for pos in range(4):
            mate_copy(pos, d).wait_send()
        for pos in (1, 2):
            near_copy(pos, d).wait_send()
            far_copy(pos, d).wait_send()
    for pos in range(4):
        core_copy(pos).wait_send()
    for axis in (1, 2):
        first_copy(axis).wait_send()
        for part in range(2):
            corner_copy(axis, part).wait_send()
            second_copy(axis, part).wait_send()


def gather_kernel(mine_ref, all_ref, send_sems, recv_sems, own_sem):
    c, e = lax.axis_index("ctx"), lax.axis_index("exp")
    count = all_ref.shape[0]
    own = pltpu.make_async_copy(mine_ref, all_ref.at[c], own_sem)
    own.start()
    barrier = pltpu.get_barrier_semaphore()
    for d in range(1, count):
        pl.semaphore_signal(
            barrier,
            inc=1,
            device_id=((c + d) % count, e),
            device_id_type=pl.DeviceIdType.MESH,
        )
    pl.semaphore_wait(barrier, count - 1)
    copies = [
        pltpu.make_async_remote_copy(
            src_ref=mine_ref,
            dst_ref=all_ref.at[c],
            send_sem=send_sems.at[d],
            recv_sem=recv_sems.at[d],
            device_id=((c + d) % count, e),
            device_id_type=pl.DeviceIdType.MESH,
        )
        for d in range(1, count)
    ]
    for item in copies:
        item.start()
    own.wait()
    for item in copies:
        item.wait()


def plane_gather(mine):
    return pl.pallas_call(
        gather_kernel,
        out_shape=jax.ShapeDtypeStruct((PLANE_CTX, *mine.shape), mine.dtype),
        in_specs=[pl.BlockSpec(memory_space=pltpu.VMEM)],
        out_specs=pl.BlockSpec(memory_space=pltpu.VMEM),
        scratch_shapes=[
            pltpu.SemaphoreType.DMA((PLANE_CTX,)),
            pltpu.SemaphoreType.DMA((PLANE_CTX,)),
            pltpu.SemaphoreType.DMA,
        ],
        compiler_params=pltpu.CompilerParams(
            collective_id=1, has_side_effects=True, vmem_limit_bytes=8 * 1024 * 1024
        ),
    )(mine)


def plane_layer(attended, hidden_in, gain, pick, spread, out_proj, gate_up, down_proj):
    blk, width = hidden_in.shape
    blocks, cap = pick.shape[0], pick.shape[1]
    units = gate_up.shape[-1]
    share, col = blk // PLANE_EXP, width // PLANE_EXP
    kind = jnp.bfloat16
    copies = 64
    return pl.pallas_call(
        layer_kernel,
        out_shape=jax.ShapeDtypeStruct((blk, col), kind),
        in_specs=[pl.BlockSpec(memory_space=pltpu.VMEM)] * 5
        + [pl.BlockSpec(memory_space=pl.ANY)] * 3,
        out_specs=pl.BlockSpec(memory_space=pltpu.VMEM),
        scratch_shapes=[
            pltpu.VMEM((width, out_proj.shape[0]), kind),
            pltpu.VMEM((2, units, width), kind),
            pltpu.VMEM((units, width), kind),
            pltpu.VMEM((blk, width), kind),
            pltpu.VMEM((blk, width), jnp.float32),
            pltpu.VMEM((PLANE_EXP, share, width), kind),
            pltpu.VMEM((share, width), jnp.float32),
            pltpu.VMEM((blocks, blk, width), kind),
            pltpu.VMEM((2 * cap, width), kind),
            pltpu.VMEM((blocks, blk, width), kind),
            pltpu.VMEM((4, blk, width), kind),
            pltpu.VMEM((2, blk // 2, width), kind),
            pltpu.VMEM((2, 2, blk // 4, width), kind),
            pltpu.VMEM((2, 2, blk // 4, width), kind),
            pltpu.VMEM((blk, width), jnp.float32),
            pltpu.VMEM((PLANE_EXP, 2, blk // 2, col), kind),
            pltpu.VMEM((PLANE_EXP, 2, blk // 2, col), kind),
            pltpu.SemaphoreType.DMA((copies,)),
            pltpu.SemaphoreType.DMA((copies,)),
            pltpu.SemaphoreType.DMA((3,)),
        ],
        compiler_params=pltpu.CompilerParams(
            collective_id=0, has_side_effects=True, vmem_limit_bytes=58 * 1024 * 1024
        ),
    )(
        attended,
        hidden_in.T,
        gain.reshape(1, width),
        pick,
        spread,
        out_proj.T,
        gate_up[0].transpose(1, 2, 0),
        down_proj[0],
    )


def per_device(
    hidden_in,
    query_input,
    key_heads_input,
    value_heads_input,
    sink_logits,
    out_proj,
    norm_gain,
    expert_ids,
    expert_gates,
    gate_up,
    down_proj,
):
    tok_rows = hidden_in.shape[0]
    ctx_count = lax.axis_size("ctx")
    exp_count = lax.axis_size("exp")
    local_heads = query_input.shape[1] // HEAD_SIZE
    token_positions = lax.axis_index("ctx") * tok_rows + jnp.arange(tok_rows, dtype=jnp.int32)
    q_rot = rotate_with_yarn(
        query_input.astype(jnp.float32).reshape(tok_rows, local_heads, HEAD_SIZE), token_positions
    ).astype(jnp.bfloat16)
    shared_key_head = lax.axis_index("exp") * local_heads // (QUERY_HEADS // KEY_VALUE_HEADS)
    key_block = lax.dynamic_slice_in_dim(key_heads_input, shared_key_head * HEAD_SIZE, HEAD_SIZE, 1)
    value_block = lax.dynamic_slice_in_dim(
        value_heads_input, shared_key_head * HEAD_SIZE, HEAD_SIZE, 1
    )
    key_rot = (
        rotate_with_yarn(
            key_block.astype(jnp.float32).reshape(tok_rows, 1, HEAD_SIZE), token_positions
        )
        .reshape(tok_rows, HEAD_SIZE)
        .astype(jnp.bfloat16)
    )
    ids_part = expert_ids.astype(jnp.bfloat16)
    gate_high = expert_gates.astype(jnp.bfloat16)
    gate_low = (expert_gates - gate_high.astype(jnp.float32)).astype(jnp.bfloat16)
    top_count = expert_ids.shape[1]
    key_value = jnp.concatenate([key_rot, value_block, ids_part, gate_high, gate_low], axis=1)
    score_scale = 1.0 / math.sqrt(HEAD_SIZE)
    in_plane = ctx_count == PLANE_CTX and exp_count == PLANE_EXP
    if in_plane:
        width = key_value.shape[1]
        padded = jnp.pad(key_value, ((0, 0), (0, -width % 128)))
        block_part = plane_gather(padded).reshape(ctx_count * tok_rows, -1)[:, :width]
    else:
        block_part = lax.all_gather(key_value, "ctx", axis=0, tiled=True)
    routing = block_part[:, 2 * HEAD_SIZE :].astype(jnp.float32)
    all_ids = routing[:, :top_count]
    all_gates = routing[:, top_count : 2 * top_count] + routing[:, 2 * top_count :]
    run_max = jnp.broadcast_to(sink_logits[:, None], (local_heads, tok_rows))
    run_total = jnp.ones((local_heads, tok_rows), jnp.float32)
    run_sum = jnp.zeros((local_heads, tok_rows, HEAD_SIZE), jnp.float32)
    key_count = block_part.shape[0]
    key_part = block_part[:, :HEAD_SIZE]
    value_part = block_part[:, HEAD_SIZE : 2 * HEAD_SIZE].astype(jnp.float32)
    scores = (
        jnp.einsum("rhd,kd->hrk", q_rot, key_part, preferred_element_type=jnp.float32) * score_scale
    )
    key_pos = jnp.arange(key_count, dtype=jnp.int32)
    visible = token_positions[:, None] >= key_pos[None, :]
    scores = jnp.where(visible[None, :, :], scores, neg_large)
    new_max = jnp.maximum(run_max, jnp.max(scores, axis=2))
    weights = jnp.exp(scores - new_max[:, :, None])
    factor = jnp.exp(run_max - new_max)
    run_total = run_total * factor + jnp.sum(weights, axis=2)
    run_sum = run_sum * factor[:, :, None] + jnp.einsum(
        "hrk,kd->hrd", weights, value_part, precision=lax.Precision.HIGHEST
    )
    run_max, run_total, run_sum = (new_max, run_total, run_sum)
    attended = (
        (run_sum / run_total[:, :, None])
        .transpose(1, 0, 2)
        .reshape(tok_rows, local_heads * HEAD_SIZE)
        .astype(jnp.bfloat16)
    )
    share_rows = tok_rows // exp_count
    my_row = lax.axis_index("exp") * share_rows
    n_experts = gate_up.shape[0] * ctx_count
    capacity = max(2, tok_rows * top_count * 5 // (4 * n_experts))
    pick, weighted = routing_matrices(all_ids, all_gates, ctx_count, tok_rows, capacity)
    if in_plane:
        return plane_layer(
            attended,
            hidden_in,
            norm_gain,
            pick,
            weighted.transpose(0, 2, 1),
            out_proj,
            gate_up,
            down_proj,
        )
    head_part = jnp.dot(attended, out_proj, preferred_element_type=jnp.float32)
    hidden_share = lax.dynamic_slice_in_dim(hidden_in, my_row, share_rows, 0)
    residual = hidden_share.astype(jnp.float32) + lax.psum_scatter(
        head_part.astype(jnp.bfloat16), "exp", scatter_dimension=0, tiled=True
    ).astype(jnp.float32)
    mean_square = jnp.mean(residual * residual, axis=1, keepdims=True)
    normed = (residual * lax.rsqrt(mean_square + 1e-05) * norm_gain[None, :]).astype(jnp.bfloat16)
    all_normed = lax.all_gather(normed, ("ctx", "exp"), axis=0, tiled=True)
    expert_rows = jnp.einsum(
        "bst,btd->bsd",
        pick,
        all_normed.reshape(ctx_count, tok_rows, D),
        preferred_element_type=jnp.float32,
    ).astype(jnp.bfloat16)
    expert_rows = expert_rows.reshape(ctx_count * capacity, D)
    unit_count = gate_up.shape[-1]
    gate_up_out = jnp.dot(
        expert_rows, gate_up.reshape(D, 2 * unit_count), preferred_element_type=jnp.float32
    )
    gate_value = gate_up_out[:, :unit_count]
    up_value = gate_up_out[:, unit_count:]
    activated = ((up_value + 1.0) * gate_value * jax.nn.sigmoid(1.702 * gate_value)).astype(
        jnp.bfloat16
    )
    partial_value = jnp.dot(
        activated, down_proj.reshape(unit_count, D), preferred_element_type=jnp.float32
    ).astype(jnp.bfloat16)
    spread = jnp.einsum(
        "bst,bsd->btd",
        weighted,
        partial_value.reshape(ctx_count, capacity, D),
        preferred_element_type=jnp.float32,
    ).astype(jnp.bfloat16)
    gated = lax.psum_scatter(
        spread.reshape(ctx_count * tok_rows, D), "ctx", scatter_dimension=0, tiled=True
    ).astype(jnp.float32)
    total = gated + lax.dynamic_update_slice_in_dim(
        jnp.zeros((tok_rows, D), jnp.float32), residual, my_row, 0
    )
    return lax.psum_scatter(
        total.astype(jnp.bfloat16), "exp", scatter_dimension=1, tiled=True
    )


def solution(mesh):
    placed = (
        P("ctx", None),
        P("ctx", "exp"),
        P("ctx", None),
        P("ctx", None),
        P("exp"),
        P("exp", None),
        P(),
        P("ctx", None),
        P("ctx", None),
        P("ctx", None, None, "exp"),
        P("ctx", "exp", None),
    )
    return jax.shard_map(
        per_device, mesh=mesh, in_specs=placed, out_specs=P("ctx", "exp"), check_vma=False
    )
```

```python
import functools
import math

import jax
import jax.numpy as jnp
import numpy as np
from jax import lax
from jax.experimental import pallas as pl
from jax.experimental.pallas import tpu as pltpu
from jax.sharding import PartitionSpec as P

D = 2880
QUERY_HEADS = 32
KEY_VALUE_HEADS = 4
HEAD_SIZE = 64


yarn_base = 150000.0
yarn_factor = 32.0
yarn_initial = 4096.0
beta_fast = 32.0
beta_slow = 1.0
neg_large = -1e30


def yarn_frequencies(head_dim):
    half_dim = head_dim // 2

    def correction(rotations):
        return (
            head_dim
            * math.log(yarn_initial / (rotations * 2.0 * math.pi))
            / (2.0 * math.log(yarn_base))
        )

    lower_dim = max(math.floor(correction(beta_fast)), 0)
    upper_dim = min(math.ceil(correction(beta_slow)), head_dim - 1)
    extrap_freq = 1.0 / yarn_base ** (np.arange(0, head_dim, 2) / head_dim)
    interp_freq = extrap_freq / yarn_factor
    ramp_part = np.clip((np.arange(half_dim) - lower_dim) / (upper_dim - lower_dim), 0.0, 1.0)
    extrap_share = 1.0 - ramp_part
    return (interp_freq * (1.0 - extrap_share) + extrap_freq * extrap_share).astype(np.float32)


def rotate_with_yarn(heads_in, token_positions):
    head_dim = heads_in.shape[-1]
    freqs = jnp.asarray(yarn_frequencies(head_dim))
    angles = token_positions.astype(jnp.float32)[:, None] * freqs[None, :]
    factor = 0.1 * math.log(yarn_factor) + 1.0
    cosine = (jnp.cos(angles) * factor)[:, None, :]
    sine = (jnp.sin(angles) * factor)[:, None, :]
    first_half = heads_in[..., : head_dim // 2]
    second_half = heads_in[..., head_dim // 2 :]
    return jnp.concatenate(
        [first_half * cosine - second_half * sine, second_half * cosine + first_half * sine],
        axis=-1,
    )


def routing_matrices(all_ids, all_gates, blocks, rows, capacity):
    mine = all_ids == lax.axis_index("ctx").astype(jnp.float32)
    chosen = jnp.sum(mine.astype(jnp.float32), axis=1).reshape(blocks, rows)
    gate = jnp.sum(jnp.where(mine, all_gates, 0.0), axis=1).reshape(blocks, rows)
    earlier = jnp.triu(jnp.ones((rows, rows), jnp.bfloat16), 1)
    slot = jnp.dot(chosen.astype(jnp.bfloat16), earlier, preferred_element_type=jnp.float32)
    place = jnp.arange(capacity, dtype=jnp.float32)[None, :, None]
    hit = (slot[:, None, :] == place) & (chosen[:, None, :] > 0.0)
    pick = hit.astype(jnp.bfloat16)
    weighted = jnp.where(hit, gate[:, None, :], 0.0).astype(jnp.bfloat16)
    return pick, weighted


PLANE_CTX = 8
PLANE_EXP = 4


def layer_kernel(
    attended_ref, hidden_ref, gain_ref, gate_ref, proj_hbm, gu_hbm, down_hbm, out_ref,
    proj, gu, down, head, hidden, zin, residual, normed, moe, core_in, first_in, corner_in,
    second_in, total, stage, zout, send_sems, recv_sems, load_sems,
):
    c, e = lax.axis_index("ctx"), lax.axis_index("exp")
    y, x, k = c // 4, c // 2 % 2, c % 2
    blk, width = head.shape
    share = blk // PLANE_EXP
    half = share // 2
    col = out_ref.shape[1]

    def at(pos, core):
        return (y + pos // 2) % 2 * 4 + (x + pos % 2) % 2 * 2 + core

    mate = at(0, 1 - k)
    ids = {}

    def copy(name, src, dst, ctx, exp):
        sem = ids.setdefault(name, len(ids))
        return pltpu.make_async_remote_copy(
            src_ref=src,
            dst_ref=dst,
            send_sem=send_sems.at[sem],
            recv_sem=recv_sems.at[sem],
            device_id=(ctx, exp),
            device_id_type=pl.DeviceIdType.MESH,
        )

    def quarter(d):
        return (e + PLANE_EXP - d) % PLANE_EXP

    def lines(axis):
        return pl.ds((axis - 1) * half, half)

    def head_copy(d):
        peer = (e + d) % PLANE_EXP
        src = head.at[pl.ds(pl.multiple_of(peer * share, share), share)]
        return copy(("head", d), src, zin.at[d], c, peer)

    def z_copy(d):
        ref = normed.at[e, c]
        return copy(("z", d), ref, ref, c, (e + d) % PLANE_EXP)

    def near_copy(pos, d):
        ref = normed.at[quarter(d), c]
        return copy(("near", pos, d), ref, ref, at(pos, k), e)

    def far_copy(pos, d):
        ref = normed.at[quarter(d), at(3 - pos, k), lines(pos)]
        return copy(("far", pos, d), ref, ref, at(pos, k), e)

    def mate_copy(pos, d):
        ref = normed.at[quarter(d), at(pos, k)]
        return copy(("mate", pos, d), ref, ref, mate, e)

    def core_copy(pos, d):
        src = moe.at[quarter(d), at(pos, 1 - k)]
        return copy(("core", pos, d), src, core_in.at[d, pos], mate, e)

    def first_copy(axis, d):
        src = moe.at[quarter(d), at(axis, k), lines(axis)]
        return copy(("first", axis, d), src, first_in.at[d, axis - 1], at(axis, k), e)

    def corner_copy(axis, d):
        src = moe.at[quarter(d), at(3, k), lines(axis)]
        return copy(("corner", axis, d), src, corner_in.at[d, axis - 1], at(axis, k), e)

    def second_copy(axis, d):
        src = moe.at[quarter(d), at(axis, k), lines(3 - axis)]
        return copy(("second", axis, d), src, second_in.at[d, axis - 1], at(axis, k), e)

    def out_copy(d, j):
        peer = (e + j) % PLANE_EXP
        return copy(("out", d, j), stage.at[d, peer], zout.at[j, quarter(d)], c, peer)

    load_proj = pltpu.make_async_copy(proj_hbm, proj, load_sems.at[2])
    load_proj.start()
    load_gu = pltpu.make_async_copy(gu_hbm, gu, load_sems.at[0])
    load_down = pltpu.make_async_copy(down_hbm, down, load_sems.at[1])
    barrier = pltpu.get_barrier_semaphore()
    friends = [(mate, e), (at(1, k), e), (at(2, k), e)]
    friends += [(c, (e + d) % PLANE_EXP) for d in (1, 2, 3)]
    for friend in friends:
        pl.semaphore_signal(
            barrier, inc=1, device_id=friend, device_id_type=pl.DeviceIdType.MESH
        )
    pl.semaphore_wait(barrier, len(friends))

    load_proj.wait()
    load_gu.start()
    load_down.start()
    across = (((1,), (1,)), ((), ()))
    head[...] = (
        lax.dot_general(proj[...], attended_ref[...], across, preferred_element_type=jnp.float32)
        .T.astype(jnp.bfloat16)
    )
    for d in (2, 1, 3):
        head_copy(d).start()
    hidden[...] = hidden_ref[...].astype(jnp.float32).T
    own_lines = pl.ds(pl.multiple_of(e * share, share), share)
    summed = hidden[own_lines, :] + head[own_lines, :].astype(jnp.float32)
    for d in (1, 3, 2):
        head_copy(d).wait_recv()
        summed = summed + zin[d].astype(jnp.float32)
    residual[...] = summed
    mean_square = jnp.mean(summed * summed, axis=1, keepdims=True)
    normed[e, c] = (summed * lax.rsqrt(mean_square + 1e-05) * gain_ref[...]).astype(jnp.bfloat16)

    def spread_near(d):
        near_copy(1, d).start()
        near_copy(2, d).start()
        mate_copy(0, d).start()

    def spread_far(d):
        for pos in (1, 2):
            near_copy(pos, d).wait_recv()
            far_copy(3 - pos, d).start()
            mate_copy(pos, d).start()

    def finish_spread(d):
        far_copy(1, d).wait_recv()
        far_copy(2, d).wait_recv()
        mate_copy(3, d).start()
        for pos in range(4):
            mate_copy(pos, d).wait_recv()

    def plus(target, added):
        target[...] = (target[...].astype(jnp.float32) + added[...].astype(jnp.float32)).astype(
            jnp.bfloat16
        )

    def sum_cores(d):
        for pos in (3, 1, 2, 0):
            core_copy(pos, d).wait_recv()
            plus(moe.at[quarter(d), at(pos, k)], core_in.at[d, pos])
            if pos == 3:
                corner_copy(1, d).start()
                corner_copy(2, d).start()
            elif pos:
                first_copy(pos, d).start()

    def sum_corners(d):
        for axis in (1, 2):
            corner_copy(axis, d).wait_recv()
            plus(
                moe.at[quarter(d), at(3 - axis, k), lines(axis)],
                corner_in.at[d, axis - 1],
            )
            second_copy(3 - axis, d).start()

    def finish_sum(d):
        for axis in (1, 2):
            first_copy(axis, d).wait_recv()
            second_copy(3 - axis, d).wait_recv()
            total[lines(axis), :] = (
                moe[quarter(d), c, lines(axis), :].astype(jnp.float32)
                + first_in[d, axis - 1].astype(jnp.float32)
                + second_in[d, 2 - axis].astype(jnp.float32)
            )
        full = total[...] + residual[...] if d == 0 else total[...]
        for f in range(PLANE_EXP):
            stage[d, f] = full[:, f * col : (f + 1) * col].astype(jnp.bfloat16)
        for j in (2, 1, 3):
            out_copy(d, j).start()

    for d in (2, 1, 3):
        z_copy(d).start()
    spread_near(0)

    def before(d):
        spread_far(d)
        if d + 1 < PLANE_EXP:
            z_copy(d + 1).wait_recv()
            spread_near(d + 1)
        finish_spread(d)
        if d == 0:
            load_gu.wait()
            load_down.wait()
        if d >= 1:
            sum_cores(d - 1)
        if d >= 2:
            finish_sum(d - 2)

    def after(d):
        for pos in (3, 1, 2, 0):
            core_copy(pos, d).start()
        if d >= 1:
            sum_corners(d - 1)

    def step(d, carry):
        for now in range(PLANE_EXP):
            pl.when(d == now)(functools.partial(before, now))
        part = quarter(d)
        tokens = normed[part].reshape(-1, width)
        gate = lax.dot_general(gu[0], tokens, across, preferred_element_type=jnp.float32)
        up = lax.dot_general(gu[1], tokens, across, preferred_element_type=jnp.float32)
        activated = (up + 1.0) * gate * jax.nn.sigmoid(1.702 * gate) * gate_ref[part]
        moe[part] = (
            jnp.dot(
                activated.T.astype(jnp.bfloat16), down[...], preferred_element_type=jnp.float32
            )
            .astype(jnp.bfloat16)
            .reshape(-1, share, width)
        )
        for now in range(PLANE_EXP):
            pl.when(d == now)(functools.partial(after, now))
        return carry

    lax.fori_loop(0, PLANE_EXP, step, 0)
    last = PLANE_EXP - 1
    sum_cores(last)
    finish_sum(last - 1)
    sum_corners(last)
    finish_sum(last)
    for d in range(PLANE_EXP):
        zout[0, quarter(d)] = stage[d, e]
        for j in (1, 2, 3):
            out_copy(d, j).wait_recv()
    for q in range(PLANE_EXP):
        result = zout[0, q].astype(jnp.float32)
        for j in (1, 2, 3):
            result = result + zout[j, q].astype(jnp.float32)
        out_ref[q * share : (q + 1) * share, :] = result.astype(jnp.bfloat16)

    for d in (1, 2, 3):
        head_copy(d).wait_send()
        z_copy(d).wait_send()
    for d in range(PLANE_EXP):
        for pos in range(4):
            mate_copy(pos, d).wait_send()
            core_copy(pos, d).wait_send()
        for pos in (1, 2):
            near_copy(pos, d).wait_send()
            far_copy(pos, d).wait_send()
            first_copy(pos, d).wait_send()
            corner_copy(pos, d).wait_send()
            second_copy(pos, d).wait_send()
        for j in (1, 2, 3):
            out_copy(d, j).wait_send()


def plane_layer(attended, hidden_in, gain, gate_rows, out_proj, gate_up, down_proj):
    blk, width = hidden_in.shape
    units = gate_up.shape[-1]
    share, col = blk // PLANE_EXP, width // PLANE_EXP
    kind = jnp.bfloat16
    copies = 96
    return pl.pallas_call(
        layer_kernel,
        out_shape=jax.ShapeDtypeStruct((blk, col), kind),
        in_specs=[pl.BlockSpec(memory_space=pltpu.VMEM)] * 4
        + [pl.BlockSpec(memory_space=pl.ANY)] * 3,
        out_specs=pl.BlockSpec(memory_space=pltpu.VMEM),
        scratch_shapes=[
            pltpu.VMEM((width, out_proj.shape[0]), kind),
            pltpu.VMEM((2, units, width), kind),
            pltpu.VMEM((units, width), kind),
            pltpu.VMEM((blk, width), kind),
            pltpu.VMEM((blk, width), jnp.float32),
            pltpu.VMEM((PLANE_EXP, share, width), kind),
            pltpu.VMEM((share, width), jnp.float32),
            pltpu.VMEM((PLANE_EXP, PLANE_CTX, share, width), kind),
            pltpu.VMEM((PLANE_EXP, PLANE_CTX, share, width), kind),
            pltpu.VMEM((PLANE_EXP, 4, share, width), kind),
            pltpu.VMEM((PLANE_EXP, 2, share // 2, width), kind),
            pltpu.VMEM((PLANE_EXP, 2, share // 2, width), kind),
            pltpu.VMEM((PLANE_EXP, 2, share // 2, width), kind),
            pltpu.VMEM((share, width), jnp.float32),
            pltpu.VMEM((PLANE_EXP, PLANE_EXP, share, col), kind),
            pltpu.VMEM((PLANE_EXP, PLANE_EXP, share, col), kind),
            pltpu.SemaphoreType.DMA((copies,)),
            pltpu.SemaphoreType.DMA((copies,)),
            pltpu.SemaphoreType.DMA((3,)),
        ],
        compiler_params=pltpu.CompilerParams(
            collective_id=0, has_side_effects=True, vmem_limit_bytes=58 * 1024 * 1024
        ),
    )(
        attended,
        hidden_in.T,
        gain.reshape(1, width),
        gate_rows,
        out_proj.T,
        gate_up[0].transpose(1, 2, 0),
        down_proj[0],
    )


def gather_kernel(mine_ref, all_ref, send_sems, recv_sems, own_sem):
    c, e = lax.axis_index("ctx"), lax.axis_index("exp")
    count = all_ref.shape[0]
    own = pltpu.make_async_copy(mine_ref, all_ref.at[c], own_sem)
    own.start()
    barrier = pltpu.get_barrier_semaphore()
    for d in range(1, count):
        pl.semaphore_signal(
            barrier,
            inc=1,
            device_id=((c + d) % count, e),
            device_id_type=pl.DeviceIdType.MESH,
        )
    pl.semaphore_wait(barrier, count - 1)
    copies = [
        pltpu.make_async_remote_copy(
            src_ref=mine_ref,
            dst_ref=all_ref.at[c],
            send_sem=send_sems.at[d],
            recv_sem=recv_sems.at[d],
            device_id=((c + d) % count, e),
            device_id_type=pl.DeviceIdType.MESH,
        )
        for d in range(1, count)
    ]
    for item in copies:
        item.start()
    own.wait()
    for item in copies:
        item.wait()


def plane_gather(mine):
    return pl.pallas_call(
        gather_kernel,
        out_shape=jax.ShapeDtypeStruct((PLANE_CTX, *mine.shape), mine.dtype),
        in_specs=[pl.BlockSpec(memory_space=pltpu.VMEM)],
        out_specs=pl.BlockSpec(memory_space=pltpu.VMEM),
        scratch_shapes=[
            pltpu.SemaphoreType.DMA((PLANE_CTX,)),
            pltpu.SemaphoreType.DMA((PLANE_CTX,)),
            pltpu.SemaphoreType.DMA,
        ],
        compiler_params=pltpu.CompilerParams(
            collective_id=1, has_side_effects=True, vmem_limit_bytes=8 * 1024 * 1024
        ),
    )(mine)


def per_device(
    hidden_in,
    query_input,
    key_heads_input,
    value_heads_input,
    sink_logits,
    out_proj,
    norm_gain,
    expert_ids,
    expert_gates,
    gate_up,
    down_proj,
):
    tok_rows = hidden_in.shape[0]
    ctx_count = lax.axis_size("ctx")
    exp_count = lax.axis_size("exp")
    local_heads = query_input.shape[1] // HEAD_SIZE
    token_positions = lax.axis_index("ctx") * tok_rows + jnp.arange(tok_rows, dtype=jnp.int32)
    q_rot = rotate_with_yarn(
        query_input.astype(jnp.float32).reshape(tok_rows, local_heads, HEAD_SIZE), token_positions
    ).astype(jnp.bfloat16)
    shared_key_head = lax.axis_index("exp") * local_heads // (QUERY_HEADS // KEY_VALUE_HEADS)
    key_block = lax.dynamic_slice_in_dim(key_heads_input, shared_key_head * HEAD_SIZE, HEAD_SIZE, 1)
    value_block = lax.dynamic_slice_in_dim(
        value_heads_input, shared_key_head * HEAD_SIZE, HEAD_SIZE, 1
    )
    key_rot = (
        rotate_with_yarn(
            key_block.astype(jnp.float32).reshape(tok_rows, 1, HEAD_SIZE), token_positions
        )
        .reshape(tok_rows, HEAD_SIZE)
        .astype(jnp.bfloat16)
    )
    ids_part = expert_ids.astype(jnp.bfloat16)
    gate_high = expert_gates.astype(jnp.bfloat16)
    gate_low = (expert_gates - gate_high.astype(jnp.float32)).astype(jnp.bfloat16)
    top_count = expert_ids.shape[1]
    score_scale = 1.0 / math.sqrt(HEAD_SIZE)
    in_plane = ctx_count == PLANE_CTX and exp_count == PLANE_EXP
    if in_plane:
        key_value = jnp.concatenate([key_rot, value_block], axis=1)
        routing = jnp.concatenate([ids_part, gate_high, gate_low], axis=1).T
        routing = jnp.pad(routing, ((0, -routing.shape[0] % 16), (0, 0)))
        gathered = plane_gather(jnp.concatenate([key_value, routing], axis=0))
        block_part = gathered[:, :tok_rows].reshape(ctx_count * tok_rows, 2 * HEAD_SIZE)
        routing = gathered[:, tok_rows:].astype(jnp.float32)
        both = (
            routing[:, top_count : 2 * top_count] + routing[:, 2 * top_count : 3 * top_count]
        )
        mine = routing[:, :top_count] == lax.axis_index("ctx").astype(jnp.float32)
        gate_rows = (
            jnp.sum(jnp.where(mine, both, 0.0), axis=1)
            .reshape(ctx_count, exp_count, tok_rows // exp_count)
            .transpose(1, 0, 2)
            .reshape(exp_count, 1, ctx_count * tok_rows // exp_count)
        )
    else:
        key_value = jnp.concatenate([key_rot, value_block, ids_part, gate_high, gate_low], axis=1)
        block_part = lax.all_gather(key_value, "ctx", axis=0, tiled=True)
        routing = block_part[:, 2 * HEAD_SIZE :].astype(jnp.float32)
        all_ids = routing[:, :top_count]
        all_gates = routing[:, top_count : 2 * top_count] + routing[:, 2 * top_count :]
    run_max = jnp.broadcast_to(sink_logits[:, None], (local_heads, tok_rows))
    run_total = jnp.ones((local_heads, tok_rows), jnp.float32)
    run_sum = jnp.zeros((local_heads, tok_rows, HEAD_SIZE), jnp.float32)
    key_count = block_part.shape[0]
    key_part = block_part[:, :HEAD_SIZE]
    value_part = block_part[:, HEAD_SIZE : 2 * HEAD_SIZE].astype(jnp.float32)
    scores = (
        jnp.einsum("rhd,kd->hrk", q_rot, key_part, preferred_element_type=jnp.float32) * score_scale
    )
    key_pos = jnp.arange(key_count, dtype=jnp.int32)
    visible = token_positions[:, None] >= key_pos[None, :]
    scores = jnp.where(visible[None, :, :], scores, neg_large)
    new_max = jnp.maximum(run_max, jnp.max(scores, axis=2))
    weights = jnp.exp(scores - new_max[:, :, None])
    factor = jnp.exp(run_max - new_max)
    run_total = run_total * factor + jnp.sum(weights, axis=2)
    run_sum = run_sum * factor[:, :, None] + jnp.einsum(
        "hrk,kd->hrd", weights, value_part, precision=lax.Precision.HIGHEST
    )
    run_max, run_total, run_sum = (new_max, run_total, run_sum)
    attended = (
        (run_sum / run_total[:, :, None])
        .transpose(1, 0, 2)
        .reshape(tok_rows, local_heads * HEAD_SIZE)
        .astype(jnp.bfloat16)
    )
    if in_plane:
        return plane_layer(
            attended, hidden_in, norm_gain, gate_rows, out_proj, gate_up, down_proj
        )
    share_rows = tok_rows // exp_count
    my_row = lax.axis_index("exp") * share_rows
    n_experts = gate_up.shape[0] * ctx_count
    capacity = max(2, tok_rows * top_count * 5 // (4 * n_experts))
    pick, weighted = routing_matrices(all_ids, all_gates, ctx_count, tok_rows, capacity)
    head_part = jnp.dot(attended, out_proj, preferred_element_type=jnp.float32)
    hidden_share = lax.dynamic_slice_in_dim(hidden_in, my_row, share_rows, 0)
    residual = hidden_share.astype(jnp.float32) + lax.psum_scatter(
        head_part.astype(jnp.bfloat16), "exp", scatter_dimension=0, tiled=True
    ).astype(jnp.float32)
    mean_square = jnp.mean(residual * residual, axis=1, keepdims=True)
    normed = (residual * lax.rsqrt(mean_square + 1e-05) * norm_gain[None, :]).astype(jnp.bfloat16)
    all_normed = lax.all_gather(normed, ("ctx", "exp"), axis=0, tiled=True)
    expert_rows = jnp.einsum(
        "bst,btd->bsd",
        pick,
        all_normed.reshape(ctx_count, tok_rows, D),
        preferred_element_type=jnp.float32,
    ).astype(jnp.bfloat16)
    expert_rows = expert_rows.reshape(ctx_count * capacity, D)
    unit_count = gate_up.shape[-1]
    gate_up_out = jnp.dot(
        expert_rows, gate_up.reshape(D, 2 * unit_count), preferred_element_type=jnp.float32
    )
    gate_value = gate_up_out[:, :unit_count]
    up_value = gate_up_out[:, unit_count:]
    activated = ((up_value + 1.0) * gate_value * jax.nn.sigmoid(1.702 * gate_value)).astype(
        jnp.bfloat16
    )
    partial_value = jnp.dot(
        activated, down_proj.reshape(unit_count, D), preferred_element_type=jnp.float32
    ).astype(jnp.bfloat16)
    spread = jnp.einsum(
        "bst,bsd->btd",
        weighted,
        partial_value.reshape(ctx_count, capacity, D),
        preferred_element_type=jnp.float32,
    ).astype(jnp.bfloat16)
    gated = lax.psum_scatter(
        spread.reshape(ctx_count * tok_rows, D), "ctx", scatter_dimension=0, tiled=True
    ).astype(jnp.float32)
    total = gated + lax.dynamic_update_slice_in_dim(
        jnp.zeros((tok_rows, D), jnp.float32), residual, my_row, 0
    )
    return lax.psum_scatter(
        total.astype(jnp.bfloat16), "exp", scatter_dimension=1, tiled=True
    )


def solution(mesh):
    placed = (
        P("ctx", None),
        P("ctx", "exp"),
        P("ctx", None),
        P("ctx", None),
        P("exp"),
        P("exp", None),
        P(),
        P("ctx", None),
        P("ctx", None),
        P("ctx", None, None, "exp"),
        P("ctx", "exp", None),
    )
    return jax.shard_map(
        per_device, mesh=mesh, in_specs=placed, out_specs=P("ctx", "exp"), check_vma=False
    )
```

```python
import functools
import math

import jax
import jax.numpy as jnp
import numpy as np
from jax import lax
from jax.experimental import pallas as pl
from jax.experimental.pallas import tpu as pltpu
from jax.sharding import PartitionSpec as P

D = 2880
QUERY_HEADS = 32
KEY_VALUE_HEADS = 4
HEAD_SIZE = 64


yarn_base = 150000.0
yarn_factor = 32.0
yarn_initial = 4096.0
beta_fast = 32.0
beta_slow = 1.0
neg_large = -1e30


def yarn_frequencies(head_dim):
    half_dim = head_dim // 2

    def correction(rotations):
        return (
            head_dim
            * math.log(yarn_initial / (rotations * 2.0 * math.pi))
            / (2.0 * math.log(yarn_base))
        )

    lower_dim = max(math.floor(correction(beta_fast)), 0)
    upper_dim = min(math.ceil(correction(beta_slow)), head_dim - 1)
    extrap_freq = 1.0 / yarn_base ** (np.arange(0, head_dim, 2) / head_dim)
    interp_freq = extrap_freq / yarn_factor
    ramp_part = np.clip((np.arange(half_dim) - lower_dim) / (upper_dim - lower_dim), 0.0, 1.0)
    extrap_share = 1.0 - ramp_part
    return (interp_freq * (1.0 - extrap_share) + extrap_freq * extrap_share).astype(np.float32)


def rotate_with_yarn(heads_in, token_positions):
    head_dim = heads_in.shape[-1]
    freqs = jnp.asarray(yarn_frequencies(head_dim))
    angles = token_positions.astype(jnp.float32)[:, None] * freqs[None, :]
    factor = 0.1 * math.log(yarn_factor) + 1.0
    cosine = (jnp.cos(angles) * factor)[:, None, :]
    sine = (jnp.sin(angles) * factor)[:, None, :]
    first_half = heads_in[..., : head_dim // 2]
    second_half = heads_in[..., head_dim // 2 :]
    return jnp.concatenate(
        [first_half * cosine - second_half * sine, second_half * cosine + first_half * sine],
        axis=-1,
    )


def routing_matrices(all_ids, all_gates, blocks, rows, capacity):
    mine = all_ids == lax.axis_index("ctx").astype(jnp.float32)
    chosen = jnp.sum(mine.astype(jnp.float32), axis=1).reshape(blocks, rows)
    gate = jnp.sum(jnp.where(mine, all_gates, 0.0), axis=1).reshape(blocks, rows)
    earlier = jnp.triu(jnp.ones((rows, rows), jnp.bfloat16), 1)
    slot = jnp.dot(chosen.astype(jnp.bfloat16), earlier, preferred_element_type=jnp.float32)
    place = jnp.arange(capacity, dtype=jnp.float32)[None, :, None]
    hit = (slot[:, None, :] == place) & (chosen[:, None, :] > 0.0)
    pick = hit.astype(jnp.bfloat16)
    weighted = jnp.where(hit, gate[:, None, :], 0.0).astype(jnp.bfloat16)
    return pick, weighted


PLANE_CTX = 8
PLANE_EXP = 4


def layer_kernel(
    attended_ref, hidden_ref, gain_ref, gate_ref, proj_hbm, gu_hbm, down_hbm, out_ref,
    proj, gu, down, head, hidden, zin, residual, normed, moe, core_in, first_in, corner_in,
    second_in, total, stage, zout, send_sems, recv_sems, load_sems,
):
    c, e = lax.axis_index("ctx"), lax.axis_index("exp")
    y, x, k = c // 4, c // 2 % 2, c % 2
    blk, width = head.shape
    share = blk // PLANE_EXP
    half = share // 2
    col = out_ref.shape[1]

    def at(pos, core):
        return (y + pos // 2) % 2 * 4 + (x + pos % 2) % 2 * 2 + core

    mate = at(0, 1 - k)
    ids = {}

    def copy(name, src, dst, ctx, exp):
        sem = ids.setdefault(name, len(ids))
        return pltpu.make_async_remote_copy(
            src_ref=src,
            dst_ref=dst,
            send_sem=send_sems.at[sem],
            recv_sem=recv_sems.at[sem],
            device_id=(ctx, exp),
            device_id_type=pl.DeviceIdType.MESH,
        )

    def quarter(d):
        return (e + PLANE_EXP - d) % PLANE_EXP

    def lines(axis):
        return pl.ds((axis - 1) * half, half)

    def head_copy(d):
        peer = (e + d) % PLANE_EXP
        src = head.at[pl.ds(pl.multiple_of(peer * share, share), share)]
        return copy(("head", d), src, zin.at[d], c, peer)

    def z_copy(d):
        ref = normed.at[e, c]
        return copy(("z", d), ref, ref, c, (e + d) % PLANE_EXP)

    def near_copy(pos, d):
        ref = normed.at[quarter(d), c]
        return copy(("near", pos, d), ref, ref, at(pos, k), e)

    def far_copy(pos, d):
        ref = normed.at[quarter(d), at(3 - pos, k), lines(pos)]
        return copy(("far", pos, d), ref, ref, at(pos, k), e)

    def mate_copy(pos, d):
        ref = normed.at[quarter(d), at(pos, k)]
        return copy(("mate", pos, d), ref, ref, mate, e)

    def core_copy(pos, d):
        src = moe.at[quarter(d), at(pos, 1 - k)]
        return copy(("core", pos, d), src, core_in.at[d, pos], mate, e)

    def first_copy(axis, d):
        src = moe.at[quarter(d), at(axis, k), lines(axis)]
        return copy(("first", axis, d), src, first_in.at[d, axis - 1], at(axis, k), e)

    def corner_copy(axis, d):
        src = moe.at[quarter(d), at(3, k), lines(axis)]
        return copy(("corner", axis, d), src, corner_in.at[d, axis - 1], at(axis, k), e)

    def second_copy(axis, d):
        src = moe.at[quarter(d), at(axis, k), lines(3 - axis)]
        return copy(("second", axis, d), src, second_in.at[d, axis - 1], at(axis, k), e)

    def out_copy(d, j):
        peer = (e + j) % PLANE_EXP
        return copy(("out", d, j), stage.at[d, peer], zout.at[j, quarter(d)], c, peer)

    load_proj = pltpu.make_async_copy(proj_hbm, proj, load_sems.at[2])
    load_proj.start()
    load_gu = pltpu.make_async_copy(gu_hbm, gu, load_sems.at[0])
    load_down = pltpu.make_async_copy(down_hbm, down, load_sems.at[1])
    barrier = pltpu.get_barrier_semaphore()
    friends = [(mate, e), (at(1, k), e), (at(2, k), e)]
    friends += [(c, (e + d) % PLANE_EXP) for d in (1, 2, 3)]
    for friend in friends:
        pl.semaphore_signal(
            barrier, inc=1, device_id=friend, device_id_type=pl.DeviceIdType.MESH
        )
    pl.semaphore_wait(barrier, len(friends))

    load_proj.wait()
    load_gu.start()
    load_down.start()
    across = (((1,), (1,)), ((), ()))
    head[...] = (
        lax.dot_general(proj[...], attended_ref[...], across, preferred_element_type=jnp.float32)
        .T.astype(jnp.bfloat16)
    )
    for d in (2, 1, 3):
        head_copy(d).start()
    hidden[...] = hidden_ref[...].astype(jnp.float32).T
    own_lines = pl.ds(pl.multiple_of(e * share, share), share)
    summed = hidden[own_lines, :] + head[own_lines, :].astype(jnp.float32)
    for d in (1, 3, 2):
        head_copy(d).wait_recv()
        summed = summed + zin[d].astype(jnp.float32)
    residual[...] = summed
    mean_square = jnp.mean(summed * summed, axis=1, keepdims=True)
    normed[e, c] = (summed * lax.rsqrt(mean_square + 1e-05) * gain_ref[...]).astype(jnp.bfloat16)

    def spread_near(d):
        near_copy(1, d).start()
        near_copy(2, d).start()
        mate_copy(0, d).start()

    def spread_far(d):
        for pos in (1, 2):
            near_copy(pos, d).wait_recv()
            far_copy(3 - pos, d).start()
            mate_copy(pos, d).start()

    def finish_spread(d):
        far_copy(1, d).wait_recv()
        far_copy(2, d).wait_recv()
        mate_copy(3, d).start()
        for pos in range(4):
            mate_copy(pos, d).wait_recv()

    def plus(target, added):
        target[...] = (target[...].astype(jnp.float32) + added[...].astype(jnp.float32)).astype(
            jnp.bfloat16
        )

    def sum_cores(d):
        for pos in (3, 1, 2, 0):
            core_copy(pos, d).wait_recv()
            plus(moe.at[quarter(d), at(pos, k)], core_in.at[d, pos])
            if pos == 3:
                corner_copy(1, d).start()
                corner_copy(2, d).start()
            elif pos:
                first_copy(pos, d).start()

    def sum_corners(d):
        for axis in (1, 2):
            corner_copy(axis, d).wait_recv()
            plus(
                moe.at[quarter(d), at(3 - axis, k), lines(axis)],
                corner_in.at[d, axis - 1],
            )
            second_copy(3 - axis, d).start()

    def finish_sum(d):
        for axis in (1, 2):
            first_copy(axis, d).wait_recv()
            second_copy(3 - axis, d).wait_recv()
            total[lines(axis), :] = (
                moe[quarter(d), c, lines(axis), :].astype(jnp.float32)
                + first_in[d, axis - 1].astype(jnp.float32)
                + second_in[d, 2 - axis].astype(jnp.float32)
            )
        full = total[...] + residual[...] if d == 0 else total[...]
        for f in range(PLANE_EXP):
            stage[d, f] = full[:, f * col : (f + 1) * col].astype(jnp.bfloat16)
        for j in (2, 1, 3):
            out_copy(d, j).start()

    order = (0, 1, 3, 2)
    z_copy(order[1]).start()
    spread_near(order[0])

    def before(i):
        spread_far(order[i])
        if i == 0:
            z_copy(order[2]).start()
        if i + 1 < PLANE_EXP:
            z_copy(order[i + 1]).wait_recv()
            spread_near(order[i + 1])
        finish_spread(order[i])
        if i == 0:
            z_copy(order[3]).start()
            load_gu.wait()
            load_down.wait()
        if i >= 1:
            sum_cores(order[i - 1])
        if i >= 2:
            finish_sum(order[i - 2])

    def after(i):
        for pos in (3, 1, 2, 0):
            core_copy(pos, order[i]).start()
        if i >= 1:
            sum_corners(order[i - 1])

    def step(i, carry):
        for now in range(PLANE_EXP):
            pl.when(i == now)(functools.partial(before, now))
        part = quarter(i + i // 2 * (5 - 2 * i))
        tokens = normed[part].reshape(-1, width)
        gate = lax.dot_general(gu[0], tokens, across, preferred_element_type=jnp.float32)
        up = lax.dot_general(gu[1], tokens, across, preferred_element_type=jnp.float32)
        activated = (up + 1.0) * gate * jax.nn.sigmoid(1.702 * gate) * gate_ref[part]
        moe[part] = (
            jnp.dot(
                activated.T.astype(jnp.bfloat16), down[...], preferred_element_type=jnp.float32
            )
            .astype(jnp.bfloat16)
            .reshape(-1, share, width)
        )
        for now in range(PLANE_EXP):
            pl.when(i == now)(functools.partial(after, now))
        return carry

    lax.fori_loop(0, PLANE_EXP, step, 0)
    sum_cores(order[3])
    finish_sum(order[2])
    sum_corners(order[3])
    finish_sum(order[3])
    for d in range(PLANE_EXP):
        zout[0, quarter(d)] = stage[d, e]
        for j in (1, 2, 3):
            out_copy(d, j).wait_recv()
    for q in range(PLANE_EXP):
        result = zout[0, q].astype(jnp.float32)
        for j in (1, 2, 3):
            result = result + zout[j, q].astype(jnp.float32)
        out_ref[q * share : (q + 1) * share, :] = result.astype(jnp.bfloat16)

    for d in (1, 2, 3):
        head_copy(d).wait_send()
        z_copy(d).wait_send()
    for d in range(PLANE_EXP):
        for pos in range(4):
            mate_copy(pos, d).wait_send()
            core_copy(pos, d).wait_send()
        for pos in (1, 2):
            near_copy(pos, d).wait_send()
            far_copy(pos, d).wait_send()
            first_copy(pos, d).wait_send()
            corner_copy(pos, d).wait_send()
            second_copy(pos, d).wait_send()
        for j in (1, 2, 3):
            out_copy(d, j).wait_send()


def plane_layer(attended, hidden_in, gain, gate_rows, out_proj, gate_up, down_proj):
    blk, width = hidden_in.shape
    units = gate_up.shape[-1]
    share, col = blk // PLANE_EXP, width // PLANE_EXP
    kind = jnp.bfloat16
    copies = 96
    return pl.pallas_call(
        layer_kernel,
        out_shape=jax.ShapeDtypeStruct((blk, col), kind),
        in_specs=[pl.BlockSpec(memory_space=pltpu.VMEM)] * 4
        + [pl.BlockSpec(memory_space=pl.ANY)] * 3,
        out_specs=pl.BlockSpec(memory_space=pltpu.VMEM),
        scratch_shapes=[
            pltpu.VMEM((width, out_proj.shape[0]), kind),
            pltpu.VMEM((2, units, width), kind),
            pltpu.VMEM((units, width), kind),
            pltpu.VMEM((blk, width), kind),
            pltpu.VMEM((blk, width), jnp.float32),
            pltpu.VMEM((PLANE_EXP, share, width), kind),
            pltpu.VMEM((share, width), jnp.float32),
            pltpu.VMEM((PLANE_EXP, PLANE_CTX, share, width), kind),
            pltpu.VMEM((PLANE_EXP, PLANE_CTX, share, width), kind),
            pltpu.VMEM((PLANE_EXP, 4, share, width), kind),
            pltpu.VMEM((PLANE_EXP, 2, share // 2, width), kind),
            pltpu.VMEM((PLANE_EXP, 2, share // 2, width), kind),
            pltpu.VMEM((PLANE_EXP, 2, share // 2, width), kind),
            pltpu.VMEM((share, width), jnp.float32),
            pltpu.VMEM((PLANE_EXP, PLANE_EXP, share, col), kind),
            pltpu.VMEM((PLANE_EXP, PLANE_EXP, share, col), kind),
            pltpu.SemaphoreType.DMA((copies,)),
            pltpu.SemaphoreType.DMA((copies,)),
            pltpu.SemaphoreType.DMA((3,)),
        ],
        compiler_params=pltpu.CompilerParams(
            collective_id=0, has_side_effects=True, vmem_limit_bytes=58 * 1024 * 1024
        ),
    )(
        attended,
        hidden_in.T,
        gain.reshape(1, width),
        gate_rows,
        out_proj.T,
        gate_up[0].transpose(1, 2, 0),
        down_proj[0],
    )


def gather_kernel(mine_ref, all_ref, send_sems, recv_sems, own_sem):
    c, e = lax.axis_index("ctx"), lax.axis_index("exp")
    count = all_ref.shape[0]
    own = pltpu.make_async_copy(mine_ref, all_ref.at[c], own_sem)
    own.start()
    barrier = pltpu.get_barrier_semaphore()
    for d in range(1, count):
        pl.semaphore_signal(
            barrier,
            inc=1,
            device_id=((c + d) % count, e),
            device_id_type=pl.DeviceIdType.MESH,
        )
    pl.semaphore_wait(barrier, count - 1)
    copies = [
        pltpu.make_async_remote_copy(
            src_ref=mine_ref,
            dst_ref=all_ref.at[c],
            send_sem=send_sems.at[d],
            recv_sem=recv_sems.at[d],
            device_id=((c + d) % count, e),
            device_id_type=pl.DeviceIdType.MESH,
        )
        for d in range(1, count)
    ]
    for item in copies:
        item.start()
    own.wait()
    for item in copies:
        item.wait()


def plane_gather(mine):
    return pl.pallas_call(
        gather_kernel,
        out_shape=jax.ShapeDtypeStruct((PLANE_CTX, *mine.shape), mine.dtype),
        in_specs=[pl.BlockSpec(memory_space=pltpu.VMEM)],
        out_specs=pl.BlockSpec(memory_space=pltpu.VMEM),
        scratch_shapes=[
            pltpu.SemaphoreType.DMA((PLANE_CTX,)),
            pltpu.SemaphoreType.DMA((PLANE_CTX,)),
            pltpu.SemaphoreType.DMA,
        ],
        compiler_params=pltpu.CompilerParams(
            collective_id=1, has_side_effects=True, vmem_limit_bytes=8 * 1024 * 1024
        ),
    )(mine)


def per_device(
    hidden_in,
    query_input,
    key_heads_input,
    value_heads_input,
    sink_logits,
    out_proj,
    norm_gain,
    expert_ids,
    expert_gates,
    gate_up,
    down_proj,
):
    tok_rows = hidden_in.shape[0]
    ctx_count = lax.axis_size("ctx")
    exp_count = lax.axis_size("exp")
    local_heads = query_input.shape[1] // HEAD_SIZE
    token_positions = lax.axis_index("ctx") * tok_rows + jnp.arange(tok_rows, dtype=jnp.int32)
    q_rot = rotate_with_yarn(
        query_input.astype(jnp.float32).reshape(tok_rows, local_heads, HEAD_SIZE), token_positions
    ).astype(jnp.bfloat16)
    shared_key_head = lax.axis_index("exp") * local_heads // (QUERY_HEADS // KEY_VALUE_HEADS)
    key_block = lax.dynamic_slice_in_dim(key_heads_input, shared_key_head * HEAD_SIZE, HEAD_SIZE, 1)
    value_block = lax.dynamic_slice_in_dim(
        value_heads_input, shared_key_head * HEAD_SIZE, HEAD_SIZE, 1
    )
    key_rot = (
        rotate_with_yarn(
            key_block.astype(jnp.float32).reshape(tok_rows, 1, HEAD_SIZE), token_positions
        )
        .reshape(tok_rows, HEAD_SIZE)
        .astype(jnp.bfloat16)
    )
    ids_part = expert_ids.astype(jnp.bfloat16)
    gate_high = expert_gates.astype(jnp.bfloat16)
    gate_low = (expert_gates - gate_high.astype(jnp.float32)).astype(jnp.bfloat16)
    top_count = expert_ids.shape[1]
    score_scale = 1.0 / math.sqrt(HEAD_SIZE)
    in_plane = ctx_count == PLANE_CTX and exp_count == PLANE_EXP
    if in_plane:
        key_value = jnp.concatenate([key_rot, value_block], axis=1)
        routing = jnp.concatenate([ids_part, gate_high, gate_low], axis=1).T
        routing = jnp.pad(routing, ((0, -routing.shape[0] % 16), (0, 0)))
        gathered = plane_gather(jnp.concatenate([key_value, routing], axis=0))
        block_part = gathered[:, :tok_rows].reshape(ctx_count * tok_rows, 2 * HEAD_SIZE)
        routing = gathered[:, tok_rows:].astype(jnp.float32)
        both = (
            routing[:, top_count : 2 * top_count] + routing[:, 2 * top_count : 3 * top_count]
        )
        mine = routing[:, :top_count] == lax.axis_index("ctx").astype(jnp.float32)
        gate_rows = (
            jnp.sum(jnp.where(mine, both, 0.0), axis=1)
            .reshape(ctx_count, exp_count, tok_rows // exp_count)
            .transpose(1, 0, 2)
            .reshape(exp_count, 1, ctx_count * tok_rows // exp_count)
        )
    else:
        key_value = jnp.concatenate([key_rot, value_block, ids_part, gate_high, gate_low], axis=1)
        block_part = lax.all_gather(key_value, "ctx", axis=0, tiled=True)
        routing = block_part[:, 2 * HEAD_SIZE :].astype(jnp.float32)
        all_ids = routing[:, :top_count]
        all_gates = routing[:, top_count : 2 * top_count] + routing[:, 2 * top_count :]
    run_max = jnp.broadcast_to(sink_logits[:, None], (local_heads, tok_rows))
    run_total = jnp.ones((local_heads, tok_rows), jnp.float32)
    run_sum = jnp.zeros((local_heads, tok_rows, HEAD_SIZE), jnp.float32)
    key_count = block_part.shape[0]
    key_part = block_part[:, :HEAD_SIZE]
    value_part = block_part[:, HEAD_SIZE : 2 * HEAD_SIZE].astype(jnp.float32)
    scores = (
        jnp.einsum("rhd,kd->hrk", q_rot, key_part, preferred_element_type=jnp.float32) * score_scale
    )
    key_pos = jnp.arange(key_count, dtype=jnp.int32)
    visible = token_positions[:, None] >= key_pos[None, :]
    scores = jnp.where(visible[None, :, :], scores, neg_large)
    new_max = jnp.maximum(run_max, jnp.max(scores, axis=2))
    weights = jnp.exp(scores - new_max[:, :, None])
    factor = jnp.exp(run_max - new_max)
    run_total = run_total * factor + jnp.sum(weights, axis=2)
    run_sum = run_sum * factor[:, :, None] + jnp.einsum(
        "hrk,kd->hrd", weights, value_part, precision=lax.Precision.HIGHEST
    )
    run_max, run_total, run_sum = (new_max, run_total, run_sum)
    attended = (
        (run_sum / run_total[:, :, None])
        .transpose(1, 0, 2)
        .reshape(tok_rows, local_heads * HEAD_SIZE)
        .astype(jnp.bfloat16)
    )
    if in_plane:
        return plane_layer(
            attended, hidden_in, norm_gain, gate_rows, out_proj, gate_up, down_proj
        )
    share_rows = tok_rows // exp_count
    my_row = lax.axis_index("exp") * share_rows
    n_experts = gate_up.shape[0] * ctx_count
    capacity = max(2, tok_rows * top_count * 5 // (4 * n_experts))
    pick, weighted = routing_matrices(all_ids, all_gates, ctx_count, tok_rows, capacity)
    head_part = jnp.dot(attended, out_proj, preferred_element_type=jnp.float32)
    hidden_share = lax.dynamic_slice_in_dim(hidden_in, my_row, share_rows, 0)
    residual = hidden_share.astype(jnp.float32) + lax.psum_scatter(
        head_part.astype(jnp.bfloat16), "exp", scatter_dimension=0, tiled=True
    ).astype(jnp.float32)
    mean_square = jnp.mean(residual * residual, axis=1, keepdims=True)
    normed = (residual * lax.rsqrt(mean_square + 1e-05) * norm_gain[None, :]).astype(jnp.bfloat16)
    all_normed = lax.all_gather(normed, ("ctx", "exp"), axis=0, tiled=True)
    expert_rows = jnp.einsum(
        "bst,btd->bsd",
        pick,
        all_normed.reshape(ctx_count, tok_rows, D),
        preferred_element_type=jnp.float32,
    ).astype(jnp.bfloat16)
    expert_rows = expert_rows.reshape(ctx_count * capacity, D)
    unit_count = gate_up.shape[-1]
    gate_up_out = jnp.dot(
        expert_rows, gate_up.reshape(D, 2 * unit_count), preferred_element_type=jnp.float32
    )
    gate_value = gate_up_out[:, :unit_count]
    up_value = gate_up_out[:, unit_count:]
    activated = ((up_value + 1.0) * gate_value * jax.nn.sigmoid(1.702 * gate_value)).astype(
        jnp.bfloat16
    )
    partial_value = jnp.dot(
        activated, down_proj.reshape(unit_count, D), preferred_element_type=jnp.float32
    ).astype(jnp.bfloat16)
    spread = jnp.einsum(
        "bst,bsd->btd",
        weighted,
        partial_value.reshape(ctx_count, capacity, D),
        preferred_element_type=jnp.float32,
    ).astype(jnp.bfloat16)
    gated = lax.psum_scatter(
        spread.reshape(ctx_count * tok_rows, D), "ctx", scatter_dimension=0, tiled=True
    ).astype(jnp.float32)
    total = gated + lax.dynamic_update_slice_in_dim(
        jnp.zeros((tok_rows, D), jnp.float32), residual, my_row, 0
    )
    return lax.psum_scatter(
        total.astype(jnp.bfloat16), "exp", scatter_dimension=1, tiled=True
    )


def solution(mesh):
    placed = (
        P("ctx", None),
        P("ctx", "exp"),
        P("ctx", None),
        P("ctx", None),
        P("exp"),
        P("exp", None),
        P(),
        P("ctx", None),
        P("ctx", None),
        P("ctx", None, None, "exp"),
        P("ctx", "exp", None),
    )
    return jax.shard_map(
        per_device, mesh=mesh, in_specs=placed, out_specs=P("ctx", "exp"), check_vma=False
    )
```
